512 devices in a mesh: seq: 64 (over z, y), tp: 8 (over x, core).
Axes of the slice: x: 4, y: 4, z: 16, core: 2. Of those that a mesh axis runs over, the one named last changes fastest.
Arguments:
- byte_states: bfloat16 [40960, 1024], P('seq')
- patch_starts: int32 [8960], P('seq'), may hold values from 0 to 640, as said below
- query_weight: bfloat16 [1024, 1024], P(None, 'tp'), may hold values from -0.1875 to 0.1875
- key_weight: bfloat16 [1024, 1024], P(None, 'tp'), may hold values from -0.1875 to 0.1875
- value_weight: bfloat16 [1024, 1024], P(None, 'tp'), may hold values from -0.1875 to 0.1875
- out_weight: bfloat16 [1024, 1024], P('tp'), may hold values from -0.1875 to 0.1875
- up_weight: bfloat16 [1024, 4096], P(None, 'tp'), may hold values from -0.09375 to 0.09375
- patch_grad: bfloat16 [5120, 4096], P('seq', 'tp'), may hold values from -6 to 6
- owner_slots: int32 [64], replicated, may hold values from 0 to 63, each once
Outputs:
- byte_grad: bfloat16 [40960, 1024], P('seq', 'tp')
- owned_grads: float32 [4096, 1024], P('seq', 'tp')
The draws below stay inside these ranges and needn't reach their ends.
Inputs may be any that keep to these rules, and one draw needn't show every extreme that they name: `patch_starts`: each device's 140 slots list in ascending order the offsets at which patches begin in its bytes, then 640 in unused slots. Byte 0 of the first device begins a patch. Every device's first patch begins before offset 128, and on some device at offset 128 - 1. Devices 2i and 2i + 1 together hold 160 patch starts; every device holds at least 20 and at most 140, and some device holds exactly 140. Device 0 holds more than 80.
All inputs are finite; a program needn't handle non-finite values.
Results may differ from the reference program's by a relative error of at most 0.04.
Values may be sent and summed in bfloat16 or wider, within the bound.
A program may use at most 64 MiB of HBM per device.

```python
import jax
import jax.numpy as jnp
from jax import lax

E = 1024
HEADS = 16
HEAD = 64
G = 4096
BYTE_DEV = 640
TAIL = 128
BLOCK_ROWS = 64
PATCH_DEV = 80
DMAX = 60
PCAP = 140
BYTES = 40960
PATCHES = 5120
BLOCKS = 64
N_SEQ = 64
N_TP = 8


def draw_byte_states(key, part):
    key = jax.random.fold_in(key, 11)
    values = jnp.clip(jax.random.normal(key, (BYTES, E), jnp.float32), -6.0, 6.0)
    return values.astype(jnp.bfloat16)


def draw_patch_starts(key, part):
    key = jax.random.fold_in(key, 5)
    devices = BYTES // BYTE_DEV
    pairs = devices // 2
    keys = jax.random.split(key, 7)
    surplus = jax.random.randint(keys[0], (pairs,), -DMAX, DMAX + 1)
    first_surplus = jax.random.randint(keys[6], (), 1, DMAX + 1)
    surplus = jnp.where(jnp.arange(pairs) == 0, first_surplus, surplus)
    chosen = jax.random.randint(keys[1], (), 0, pairs)
    direction = jax.random.randint(keys[2], (), 0, 2) * 2 - 1
    direction = jnp.where(chosen == 0, 1, direction)
    surplus = jnp.where(jnp.arange(pairs) == chosen, direction * DMAX, surplus)
    totals = jnp.stack([PATCH_DEV + surplus, PATCH_DEV - surplus], axis=1).reshape(devices)
    firsts = jax.random.randint(keys[3], (devices,), 0, TAIL)
    late = jax.random.randint(keys[4], (), 1, devices)
    firsts = jnp.where(jnp.arange(devices) == late, TAIL - 1, firsts)
    firsts = jnp.where(jnp.arange(devices) == 0, 0, firsts)
    device_keys = jax.random.split(keys[5], devices)

    def one_device(dev_key, first_pos, total):
        ranks = jax.random.permutation(dev_key, BYTE_DEV)
        positions = jnp.arange(BYTE_DEV)
        ordering = jnp.where(positions > first_pos, ranks, BYTE_DEV + positions)
        picked = jnp.argsort(ordering)[:PCAP - 1]
        slot_ids = jnp.arange(PCAP - 1)
        picked = jnp.where(slot_ids < total - 1, picked, BYTE_DEV)
        return jnp.sort(jnp.concatenate([first_pos[None], picked]))
    return jax.vmap(one_device)(device_keys, firsts, totals).reshape(-1).astype(jnp.int32)


def shard_levels(own_key, dims, cuts, smallest, high):
    def one(position, shards_of):
        draws = jax.random.uniform(jax.random.fold_in(jax.random.fold_in(own_key, 6), position), (shards_of,), jnp.float32, smallest / len(cuts), high / len(cuts))
        return jnp.repeat(jnp.exp(draws), dims[position] // shards_of).reshape((-1,) + (1,) * (len(dims) - position - 1))

    level = one(*cuts[0])
    for cut in cuts[1:]:
        level = level * one(*cut)
    return level


def normal_values(own_key, shape, deviation, limit, cuts=(), kind=jnp.bfloat16):
    loudness = shard_levels(own_key, shape, cuts, -0.22, 0.18) if cuts else 1.0
    drawn = jax.random.normal(own_key, shape, jnp.float32) * deviation * loudness
    return jnp.minimum(jnp.maximum(drawn, -limit), limit).astype(kind)


def setup_inputs(seed: int = 0) -> dict:
    streams_of = jax.random.split(jax.random.key(seed), 10)
    byte_states = draw_byte_states(jax.random.fold_in(streams_of[9], 71), 0)
    patch_starts = draw_patch_starts(jax.random.fold_in(streams_of[9], 71), 0)
    query_weight = normal_values(streams_of[2], (E, E), E ** -0.5, 0.1875, ((1, 8),))
    key_weight = normal_values(streams_of[3], (E, E), E ** -0.5, 0.1875, ((1, 8),))
    value_weight = normal_values(streams_of[4], (E, E), E ** -0.5, 0.1875, ((1, 8),))
    out_weight = normal_values(streams_of[5], (E, E), E ** -0.5, 0.1875, ((0, 8),))
    up_weight = normal_values(streams_of[6], (E, G), G ** -0.5, 0.09375, ((1, 8),))
    patch_grad = normal_values(streams_of[7], (PATCHES, G), 1.0, 6.0, ((0, 64), (1, 8)))
    owner_slots = jax.random.permutation(streams_of[8], BLOCKS).astype(jnp.int32)
    return {"byte_states": byte_states, "patch_starts": patch_starts, "query_weight": query_weight, "key_weight": key_weight, "value_weight": value_weight, "out_weight": out_weight, "up_weight": up_weight, "patch_grad": patch_grad, "owner_slots": owner_slots}


def reference(byte_states, patch_starts, query_weight, key_weight, value_weight, out_weight, up_weight, patch_grad, owner_slots):
    fp = jnp.float32
    bf = jnp.bfloat16
    patches = PATCH_DEV * N_SEQ
    total_bytes = BYTE_DEV * N_SEQ
    starts = patch_starts.reshape(N_SEQ, PCAP)
    base = (jnp.arange(N_SEQ, dtype=jnp.int32) * BYTE_DEV)[:, None]
    marked = jnp.where(starts < BYTE_DEV, starts + base, total_bytes).reshape(-1).astype(jnp.int32)
    flags = jnp.zeros((total_bytes,), jnp.int32).at[marked].add(1, mode="drop")
    segment_of = (jnp.cumsum(flags) - 1).astype(jnp.int32)
    counts = jax.ops.segment_sum(jnp.ones((total_bytes,), fp), segment_of, patches)
    pooled = (jax.ops.segment_sum(byte_states.astype(fp), segment_of, patches) / counts[:, None]).astype(bf)
    scale = HEAD ** -0.5
    queries = jnp.dot(pooled, query_weight, preferred_element_type=fp).astype(bf)
    key_rows = jnp.dot(byte_states, key_weight, preferred_element_type=fp).astype(bf)
    value_rows = jnp.dot(byte_states, value_weight, preferred_element_type=fp).astype(bf)
    query_bytes = queries[segment_of].astype(fp)
    scores = (query_bytes * key_rows.astype(fp)).reshape(total_bytes, HEADS, HEAD).sum(-1) * scale
    patch_max = jax.ops.segment_max(scores, segment_of, patches)
    expo = jnp.exp(scores - patch_max[segment_of])
    denom = jax.ops.segment_sum(expo, segment_of, patches)
    weights = expo / denom[segment_of]
    weights_bf = lax.optimization_barrier(weights.astype(bf))
    weights_wide = jnp.repeat(weights_bf.astype(fp), HEAD, axis=1)
    attended = jax.ops.segment_sum(weights_wide * value_rows.astype(fp), segment_of, patches).astype(bf)
    grad_mix = jnp.dot(patch_grad, up_weight.T, preferred_element_type=fp)
    mix_bf = grad_mix.astype(bf)
    grad_attended = jnp.dot(mix_bf, out_weight.T, preferred_element_type=fp).astype(bf)
    out_grad_t = jnp.dot(mix_bf.T, attended, preferred_element_type=fp)
    delta = (grad_attended.astype(fp) * attended.astype(fp)).reshape(patches, HEADS, HEAD).sum(-1)
    grad_bytes = grad_attended[segment_of].astype(fp)
    grad_weights = (grad_bytes * value_rows.astype(fp)).reshape(total_bytes, HEADS, HEAD).sum(-1)
    grad_scores = weights * (grad_weights - delta[segment_of])
    grad_values = (weights_wide * grad_bytes).astype(bf)
    score_wide = jnp.repeat(grad_scores, HEAD, axis=1)
    grad_keys = (score_wide * query_bytes * scale).astype(bf)
    grad_queries = (jax.ops.segment_sum(score_wide * key_rows.astype(fp), segment_of, patches) * scale).astype(bf)
    key_grad = jnp.dot(byte_states.T, grad_keys, preferred_element_type=fp)
    value_grad = jnp.dot(byte_states.T, grad_values, preferred_element_type=fp)
    query_grad = jnp.dot(pooled.T, grad_queries, preferred_element_type=fp)
    group_cols = E // N_TP
    summed = jnp.zeros((total_bytes, E), fp)
    for group in range(N_TP):
        low = group * group_cols
        high = low + group_cols
        pooled_back = jnp.dot(grad_queries[:, low:high], query_weight[:, low:high].T, preferred_element_type=fp) / counts[:, None]
        partial_value = jnp.dot(grad_keys[:, low:high], key_weight[:, low:high].T, preferred_element_type=fp)
        partial_value = partial_value + jnp.dot(grad_values[:, low:high], value_weight[:, low:high].T, preferred_element_type=fp)
        partial_value = partial_value + pooled_back[segment_of]
        summed = summed + lax.optimization_barrier(partial_value.astype(bf)).astype(fp)
    byte_grad = (summed + (grad_mix / counts[:, None])[segment_of]).astype(bf)
    stacked = jnp.stack([query_grad, key_grad, value_grad, out_grad_t]).reshape(BLOCKS, BLOCK_ROWS, E)
    owned_grads = stacked[owner_slots].reshape(4 * E, E)
    return byte_grad, owned_grads
```

```python
import functools

import jax
import jax.numpy as jnp
from jax import lax
from jax.experimental import pallas as pl
from jax.experimental.pallas import tpu as pltpu
from jax.sharding import PartitionSpec as P

HEAD = 64
NY = 4
NEG = -1e30
F32 = jnp.float32
BF = jnp.bfloat16
NT = (((1,), (1,)), ((), ()))
TN = (((0,), (0,)), ((), ()))


def dot(a, b, dims=(((1,), (0,)), ((), ()))):
    return lax.dot_general(a, b, dims, preferred_element_type=F32)


def up16(n):
    return -(-n // 16) * 16


def row_of(mask, value):
    return jnp.sum(jnp.where(mask, value, 0.0), axis=0, keepdims=True)


def rows8(width, *rows):
    index = lax.broadcasted_iota(jnp.int32, (8, width), 0)
    out = jnp.zeros((8, width), F32)
    for i, row in enumerate(rows):
        out = jnp.where(index == i, row, out)
    return out


def z_order(nz):
    return sorted(range(1, nz), key=lambda d: -min(d, nz - d)) + [0]


def kernel(
    sizes,
    cols_ref, rows_ref, slots_ref, bytes_hbm, wq_hbm, wk_hbm, wv_hbm, wo_hbm, up_hbm, pg_hbm,
    byte_out, owned_out,
    bytes_ref, wq_ref, wk_ref, wv_ref, wo_ref, up_ref, pg_ref,
    bytes_t, k_ref, v_ref, pooled_ref, pooled_t, mt_ref, mix_ref, pb_ref, stack_ref,
    gm_send, gm_recv, mix_own, mix_prev, mix_next, mix_blk,
    a_send, a_recv, b_send, b_recv, d_send, d_recv,
    part_send, part_recv, part_own, y_send, y_recv, z_send, z_recv,
    load_sem, gm_ssem, gm_rsem, m_ssem, m_rsem, ag_ssem, ag_rsem,
    a_ssem, a_rsem, b_ssem, b_rsem, d_ssem, d_rsem,
    p_ssem, p_rsem, y_ssem, y_rsem, z_ssem, z_rsem,
):
    n_seq, ntp, pcap, rows_dev, window, chunks = sizes
    nz = n_seq // NY
    slots = mt_ref.shape[1]
    byte_dev, width = bytes_ref.shape
    cols = k_ref.shape[1]
    block = owned_out.shape[0]
    scale = HEAD ** -0.5
    s = lax.axis_index("seq")
    t = lax.axis_index("tp")
    y, z = lax.rem(s, NY), s // NY
    following, before = lax.rem(s + 1, n_seq), lax.rem(s + n_seq - 1, n_seq)
    order = z_order(nz)

    def tp_peer(o):
        return lax.rem(t + o, ntp)

    def y_peer(o):
        return z * NY + lax.rem(y + o, NY)

    def z_peer(o):
        return lax.rem(z + o, nz) * NY + y

    def send(src, dst, ssem, rsem, **where):
        return pltpu.make_async_remote_copy(
            src_ref=src, dst_ref=dst, send_sem=ssem, recv_sem=rsem,
            device_id=where, device_id_type=pl.DeviceIdType.MESH,
        )

    barrier = pltpu.get_barrier_semaphore()
    peers = [{"tp": tp_peer(o)} for o in range(1, ntp)]
    peers += [{"seq": following}, {"seq": before}]
    peers += [{"seq": y_peer(o)} for o in range(1, NY)]
    peers += [{"seq": z_peer(o)} for o in range(1, nz)]
    for peer in peers:
        pl.semaphore_signal(barrier, inc=1, device_id=peer, device_id_type=pl.DeviceIdType.MESH)

    loads = [
        pltpu.make_async_copy(src, dst, load_sem.at[i])
        for i, (src, dst) in enumerate([
            (pg_hbm, pg_ref), (up_hbm, up_ref), (bytes_hbm, bytes_ref), (wk_hbm, wk_ref),
            (wv_hbm, wv_ref), (wq_hbm, wq_ref), (wo_hbm, wo_ref),
        ])
    ]
    for load in loads:
        load.start()

    lo, hi = cols_ref[:, 0:1], cols_ref[:, 1:2]
    position = lax.broadcasted_iota(jnp.int32, (slots, byte_dev), 1)
    member = (position >= lo) & (position < hi)
    member_bf = jnp.where(member, 1.0, 0.0).astype(BF)
    position_t = lax.broadcasted_iota(jnp.int32, (byte_dev, slots), 0)
    member_t = (position_t >= rows_ref[0:1, :]) & (position_t < rows_ref[1:2, :])
    mt_ref[...] = jnp.where(member_t, 1.0, 0.0).astype(BF)
    slot = lax.broadcasted_iota(jnp.int32, (slots, 1), 0)
    used = (slot < pcap) & (lo < byte_dev)
    owned = jnp.sum(jnp.where(used, 1.0, 0.0), axis=0, keepdims=True).astype(jnp.int32)
    is_prev = slot == pcap
    is_last = slot == owned - 1
    count_own = (hi - lo).astype(F32)
    base = jnp.where(lax.rem(s, 2) == 0, 0, rows_dev - owned)
    wanted = base + jnp.where(is_prev, -1, slot)

    def select(first, size):
        row = lax.broadcasted_iota(jnp.int32, (slots, size), 1) + first
        return jnp.where((row == wanted) & (used | is_prev), 1.0, 0.0).astype(BF)

    loads[0].wait()
    loads[1].wait()
    pg = pg_ref[...]

    def mix_partial(j):
        return dot(pg, up_ref[pl.ds(pl.multiple_of(j * cols, cols), cols), :], NT)

    for o in range(1, ntp):
        gm_send[o - 1] = mix_partial(tp_peer(o)).astype(BF)
    pl.semaphore_wait(barrier, len(peers))
    gm_copies = [
        send(gm_send.at[o - 1], gm_recv.at[o - 1], gm_ssem.at[o - 1], gm_rsem.at[o - 1], tp=tp_peer(o))
        for o in range(1, ntp)
    ]
    for copy in gm_copies:
        copy.start()
    gm_own = mix_partial(t)

    def exchange(src, dst, ssem, rsem):
        copies = [
            send(src.at[0], dst.at[0], ssem.at[0], rsem.at[0], seq=following),
            send(src.at[1], dst.at[1], ssem.at[1], rsem.at[1], seq=before),
        ]
        for copy in copies:
            copy.start()
        return copies

    loads[2].wait()
    pooled_sum = dot(member_bf, bytes_ref[...])
    count_row = jnp.broadcast_to(row_of(is_last, count_own), (1, width))
    a_send[0] = rows8(width, row_of(is_last, pooled_sum), count_row)
    count_row = jnp.broadcast_to(row_of(is_prev, count_own), (1, width))
    a_send[1] = rows8(width, row_of(is_prev, pooled_sum), count_row)
    a_copies = exchange(a_send, a_recv, a_ssem, a_rsem)

    loads[3].wait()
    k_ref[...] = dot(bytes_ref[...], wk_ref[...]).astype(BF)
    loads[4].wait()
    v_ref[...] = dot(bytes_ref[...], wv_ref[...]).astype(BF)

    for copy in gm_copies:
        copy.wait()
    total = gm_own
    for o in range(1, ntp):
        total = total + gm_recv[o - 1].astype(F32)
    mix_own[...] = total.astype(BF)
    m_copies = [
        send(mix_own.at[pl.ds(rows_dev - window, window)], mix_prev, m_ssem.at[0], m_rsem.at[0], seq=following),
        send(mix_own.at[pl.ds(0, window)], mix_next, m_ssem.at[1], m_rsem.at[1], seq=before),
    ]
    for copy in m_copies:
        copy.start()

    for copy in a_copies:
        copy.wait()
    lane = lax.broadcasted_iota(jnp.int32, (1, cols), 1)
    head0 = lane < HEAD

    def merged(own, received, index):
        width_here = own.shape[1]
        extra = jnp.where(is_prev, received[0, index:index + 1, 0:width_here], 0.0)
        return own + extra + jnp.where(is_last, received[1, index:index + 1, 0:width_here], 0.0)

    pooled_sum = merged(pooled_sum, a_recv, 0)
    counts = jnp.maximum(merged(count_own, a_recv, 1), 1.0)
    pooled_ref[...] = (pooled_sum / counts).astype(BF)
    loads[5].wait()
    queries = dot(pooled_ref[...], wq_ref[...]).astype(BF)

    for copy in m_copies:
        copy.wait()
    picked = dot(select(0, rows_dev), mix_own[...])
    picked = picked + dot(select(-window, window), mix_prev[...])
    picked = picked + dot(select(rows_dev, window), mix_next[...])
    mix_blk[...] = picked.astype(BF)
    mine = pl.ds(pl.multiple_of(t * cols, cols), cols)
    ag_copies = [
        send(mix_blk, mix_ref.at[:, mine], ag_ssem.at[o - 1], ag_rsem.at[o - 1], tp=tp_peer(o))
        for o in range(1, ntp)
    ]
    for copy in ag_copies:
        copy.start()
    mix_ref[:, mine] = mix_blk[...]

    def heads(value):
        zero = jnp.zeros_like(value)
        return jnp.concatenate([jnp.where(head0, value, zero), jnp.where(head0, zero, value)], axis=0)

    def unheads(value):
        return jnp.where(head0, value[:slots], value[slots:])

    member2 = jnp.concatenate([member, member], axis=0)
    queries2 = heads(queries)
    scores = jnp.where(member2, dot(queries2, k_ref[...], NT) * scale, NEG)
    peak = jnp.max(scores, axis=1, keepdims=True)
    expo = jnp.where(member2, jnp.exp(scores - peak), 0.0)
    sums = unheads(jnp.sum(expo, axis=1, keepdims=True))
    peaks = unheads(peak)
    partial_out = unheads(dot(expo.astype(BF), v_ref[...]))
    for i, mask in enumerate((is_last, is_prev)):
        b_send[i] = rows8(cols, row_of(mask, partial_out), row_of(mask, peaks), row_of(mask, sums))
    b_copies = exchange(b_send, b_recv, b_ssem, b_rsem)
    bytes_t[...] = bytes_ref[...].T
    pooled_t[...] = pooled_ref[...].T
    for copy in b_copies:
        copy.wait()

    def received(index, empty):
        other = jnp.where(is_last, b_recv[1, index:index + 1, :], empty)
        return jnp.where(is_prev, b_recv[0, index:index + 1, :], other)

    other_peaks = received(1, NEG)
    top = jnp.maximum(peaks, other_peaks)
    keep, add = jnp.exp(peaks - top), jnp.exp(other_peaks - top)
    denom = sums * keep + received(2, 0.0) * add
    denom = jnp.where(denom > 0.0, denom, 1.0)
    attended = ((partial_out * keep + received(0, 0.0) * add) / denom).astype(BF)
    factor = keep / denom
    factor2 = jnp.concatenate([factor[:, 0:1], factor[:, HEAD:HEAD + 1]], axis=0)
    weights = expo * factor2

    def stack(i, value):
        count = width // block
        stack_ref[pl.ds(i * count, count)] = value.astype(BF).reshape(count, block, cols)

    loads[6].wait()
    for copy in ag_copies:
        copy.wait()
    grad_attended = dot(mix_ref[...], wo_ref[...], NT).astype(BF)
    grad2 = heads(grad_attended)
    delta = jnp.sum(grad2.astype(F32) * heads(attended).astype(F32), axis=1, keepdims=True)
    grad_scores = (weights * (dot(grad2, v_ref[...], NT) - delta)).astype(BF)
    grad_queries = unheads(dot(grad_scores, k_ref[...])) * scale
    for i, mask in enumerate((is_last, is_prev)):
        d_send[i] = rows8(cols, row_of(mask, grad_queries))
    d_copies = exchange(d_send, d_recv, d_ssem, d_rsem)
    grad_keys = (dot(grad_scores, queries2, TN) * scale).astype(BF)
    grad_values = dot(weights.astype(BF), grad2, TN).astype(BF)
    stack(1, dot(bytes_t[...], grad_keys))
    stack(2, dot(bytes_t[...], grad_values))
    counted = jnp.where(is_prev, jnp.zeros_like(attended), attended)
    stack(3, dot(mix_ref[...], counted, TN))
    for copy in d_copies:
        copy.wait()
    grad_queries = merged(grad_queries, d_recv, 0).astype(BF)
    counted = jnp.where(is_prev, jnp.zeros_like(grad_queries), grad_queries)
    stack(0, dot(pooled_t[...], counted))

    per = block * nz // chunks
    for i, o in enumerate(order):
        target = lax.rem(z + o, nz) * NY

        def reorder(q, _, i=i, target=target):
            y_send[q, pl.ds(i * block, block), :] = stack_ref[slots_ref[target + q]]
            return 0

        lax.fori_loop(0, NY, reorder, 0)
    y_copies = []
    for c in range(chunks):
        part = pl.ds(c * per, per)
        y_copies.append([
            send(
                y_send.at[lax.rem(y + o, NY), part], y_recv.at[o - 1, part],
                y_ssem.at[o - 1, c], y_rsem.at[o - 1, c], seq=y_peer(o),
            )
            for o in range(1, NY)
        ])
        for copy in y_copies[-1]:
            copy.start()

    pb_ref[...] = (dot(grad_queries, wq_ref[...], NT) / counts).astype(BF)

    def byte_partial(j):
        columns = pl.ds(pl.multiple_of(j * cols, cols), cols)
        value = dot(grad_keys, wk_ref[columns, :], NT) + dot(grad_values, wv_ref[columns, :], NT)
        return value + dot(mt_ref[...], pb_ref[:, columns])

    p_copies = []
    for o in range(1, ntp):
        part_send[o - 1] = byte_partial(tp_peer(o)).astype(BF)
        p_copies.append(send(
            part_send.at[o - 1], part_recv.at[o - 1], p_ssem.at[o - 1], p_rsem.at[o - 1], tp=tp_peer(o),
        ))
        p_copies[-1].start()
    mix_mean = (mix_blk[...].astype(F32) / counts).astype(BF)
    part_own[...] = byte_partial(t) + dot(mt_ref[...], mix_mean)

    z_copies = []
    for c in range(chunks):
        for copy in y_copies[c]:
            copy.wait()
        part = pl.ds(c * per, per)
        summed = y_send[y, part, :].astype(F32)
        for o in range(1, NY):
            summed = summed + y_recv[o - 1, part, :].astype(F32)
        z_send[part, :] = summed.astype(BF)
        for i in range(c * nz // chunks, (c + 1) * nz // chunks):
            if order[i]:
                z_copies.append(send(
                    z_send.at[pl.ds(i * block, block)], z_recv.at[i], z_ssem.at[i], z_rsem.at[i],
                    seq=z_peer(order[i]),
                ))
                z_copies[-1].start()

    total = part_own[...]
    for o in range(1, ntp):
        p_copies[o - 1].wait()
        total = total + part_recv[o - 1].astype(F32)
    byte_out[...] = total.astype(BF)

    total = z_send[pl.ds((nz - 1) * block, block), :].astype(F32)
    for i, copy in enumerate(z_copies):
        copy.wait()
        total = total + z_recv[i].astype(F32)
    owned_out[...] = total


def local(
    byte_states, patch_starts, query_weight, key_weight, value_weight, out_weight, up_weight, patch_grad,
    owner_slots, *, n_seq, ntp,
):
    byte_dev, width = byte_states.shape
    pcap = patch_starts.shape[0]
    rows_dev, features = patch_grad.shape
    cols = query_weight.shape[1]
    slots = up16(pcap + 1)
    window = up16(pcap - rows_dev + 1)
    nz = n_seq // NY
    chunks = 4 if nz % 4 == 0 else nz
    block = 4 * width // n_seq
    fill = jnp.full((slots - pcap - 1,), byte_dev, jnp.int32)
    lo = jnp.concatenate([patch_starts, jnp.zeros((1,), jnp.int32), fill])
    hi = jnp.concatenate([patch_starts[1:], jnp.full((1,), byte_dev, jnp.int32), patch_starts[:1], fill])
    edges = jnp.stack([lo, hi])
    vmem = pl.BlockSpec(memory_space=pltpu.VMEM)
    hbm = pl.BlockSpec(memory_space=pl.ANY)
    dma = pltpu.SemaphoreType.DMA
    pairs = [dma((2,))] * 2
    return pl.pallas_call(
        functools.partial(kernel, (n_seq, ntp, pcap, rows_dev, window, chunks)),
        out_shape=(
            jax.ShapeDtypeStruct((byte_dev, cols), BF),
            jax.ShapeDtypeStruct((block, cols), F32),
        ),
        in_specs=[vmem, vmem, pl.BlockSpec(memory_space=pltpu.SMEM)] + [hbm] * 7,
        out_specs=(vmem, vmem),
        scratch_shapes=[
            pltpu.VMEM((byte_dev, width), BF),
            pltpu.VMEM((width, cols), BF),
            pltpu.VMEM((width, cols), BF),
            pltpu.VMEM((width, cols), BF),
            pltpu.VMEM((cols, width), BF),
            pltpu.VMEM((width, features), BF),
            pltpu.VMEM((rows_dev, features), BF),
            pltpu.VMEM((width, byte_dev), BF),
            pltpu.VMEM((byte_dev, cols), BF),
            pltpu.VMEM((byte_dev, cols), BF),
            pltpu.VMEM((slots, width), BF),
            pltpu.VMEM((width, slots), BF),
            pltpu.VMEM((byte_dev, slots), BF),
            pltpu.VMEM((slots, width), BF),
            pltpu.VMEM((slots, width), BF),
            pltpu.VMEM((n_seq, block, cols), BF),
            pltpu.VMEM((ntp - 1, rows_dev, cols), BF),
            pltpu.VMEM((ntp - 1, rows_dev, cols), BF),
            pltpu.VMEM((rows_dev, cols), BF),
            pltpu.VMEM((window, cols), BF),
            pltpu.VMEM((window, cols), BF),
            pltpu.VMEM((slots, cols), BF),
            pltpu.VMEM((2, 8, width), F32),
            pltpu.VMEM((2, 8, width), F32),
            pltpu.VMEM((2, 8, cols), F32),
            pltpu.VMEM((2, 8, cols), F32),
            pltpu.VMEM((2, 8, cols), F32),
            pltpu.VMEM((2, 8, cols), F32),
            pltpu.VMEM((ntp - 1, byte_dev, cols), BF),
            pltpu.VMEM((ntp - 1, byte_dev, cols), BF),
            pltpu.VMEM((byte_dev, cols), F32),
            pltpu.VMEM((NY, nz * block, cols), BF),
            pltpu.VMEM((NY - 1, nz * block, cols), BF),
            pltpu.VMEM((nz * block, cols), BF),
            pltpu.VMEM((nz - 1, block, cols), BF),
            dma((7,)),
            dma((ntp - 1,)), dma((ntp - 1,)),
            *pairs,
            dma((ntp - 1,)), dma((ntp - 1,)),
            *pairs, *pairs, *pairs,
            dma((ntp - 1,)), dma((ntp - 1,)),
            dma((NY - 1, chunks)), dma((NY - 1, chunks)),
            dma((nz - 1,)), dma((nz - 1,)),
        ],
        compiler_params=pltpu.CompilerParams(
            collective_id=0, has_side_effects=True, vmem_limit_bytes=48 * 1024 * 1024
        ),
    )(
        edges.T, jnp.pad(edges, ((0, 6), (0, 0))), owner_slots, byte_states, query_weight, key_weight,
        value_weight, out_weight, up_weight, patch_grad,
    )


def solution(mesh):
    in_specs = (
        P("seq", None),
        P("seq"),
        P(None, "tp"),
        P(None, "tp"),
        P(None, "tp"),
        P("tp", None),
        P(None, "tp"),
        P("seq", "tp"),
        P(),
    )
    out_specs = (P("seq", "tp"), P("seq", "tp"))
    step = functools.partial(local, n_seq=mesh.shape["seq"], ntp=mesh.shape["tp"])
    return jax.shard_map(step, mesh=mesh, in_specs=in_specs, out_specs=out_specs, check_vma=False)
```

```python
import functools

import jax
import jax.numpy as jnp
from jax import lax
from jax.experimental import pallas as pl
from jax.experimental.pallas import tpu as pltpu
from jax.sharding import PartitionSpec as P

HEAD = 64
NY = 4
NEG = -1e30
F32 = jnp.float32
BF = jnp.bfloat16
NT = (((1,), (1,)), ((), ()))
TN = (((0,), (0,)), ((), ()))


def dot(a, b, dims=(((1,), (0,)), ((), ()))):
    return lax.dot_general(a, b, dims, preferred_element_type=F32)


def up16(n):
    return -(-n // 16) * 16


def row_of(mask, value):
    return jnp.sum(jnp.where(mask, value, 0.0), axis=0, keepdims=True)


def rows8(width, *rows):
    index = lax.broadcasted_iota(jnp.int32, (8, width), 0)
    out = jnp.zeros((8, width), F32)
    for i, row in enumerate(rows):
        out = jnp.where(index == i, row, out)
    return out


def z_order(nz):
    return sorted(range(1, nz), key=lambda d: -min(d, nz - d)) + [0]


def kernel(
    sizes,
    starts_ref, slots_ref, bytes_hbm, wq_hbm, wk_hbm, wv_hbm, wo_hbm, up_hbm, pg_hbm,
    byte_out, owned_out,
    bytes_ref, wq_ref, wk_ref, wv_ref, wo_ref, up_ref, pg_ref,
    bytes_t, k_ref, v_ref, pooled_ref, pooled_t, mt_ref, mix_ref, pb_ref, stack_ref,
    gm_send, gm_recv, mix_own, mix_prev, mix_next, mix_blk,
    a_send, a_recv, b_send, b_recv, d_send, d_recv,
    part_send, part_recv, part_own, y_send, y_recv, z_send, z_recv,
    load_sem, gm_ssem, gm_rsem, m_ssem, m_rsem, ag_ssem, ag_rsem,
    a_ssem, a_rsem, b_ssem, b_rsem, d_ssem, d_rsem,
    p_ssem, p_rsem, y_ssem, y_rsem, z_ssem, z_rsem,
):
    n_seq, ntp, pcap, rows_dev, window, chunks = sizes
    nz = n_seq // NY
    slots = mt_ref.shape[1]
    byte_dev, width = bytes_ref.shape
    cols = k_ref.shape[1]
    block = owned_out.shape[0]
    scale = HEAD ** -0.5
    s = lax.axis_index("seq")
    t = lax.axis_index("tp")
    y, z = lax.rem(s, NY), s // NY
    following, before = lax.rem(s + 1, n_seq), lax.rem(s + n_seq - 1, n_seq)
    order = z_order(nz)

    def tp_peer(o):
        return lax.rem(t + o, ntp)

    def y_peer(o):
        return z * NY + lax.rem(y + o, NY)

    def z_peer(o):
        return lax.rem(z + o, nz) * NY + y

    def send(src, dst, ssem, rsem, **where):
        return pltpu.make_async_remote_copy(
            src_ref=src, dst_ref=dst, send_sem=ssem, recv_sem=rsem,
            device_id=where, device_id_type=pl.DeviceIdType.MESH,
        )

    barrier = pltpu.get_barrier_semaphore()
    peers = [{"tp": tp_peer(o)} for o in range(1, ntp)]
    peers += [{"seq": following}, {"seq": before}]
    peers += [{"seq": y_peer(o)} for o in range(1, NY)]
    peers += [{"seq": z_peer(o)} for o in range(1, nz)]
    for peer in peers:
        pl.semaphore_signal(barrier, inc=1, device_id=peer, device_id_type=pl.DeviceIdType.MESH)

    loads = [
        pltpu.make_async_copy(src, dst, load_sem.at[i])
        for i, (src, dst) in enumerate([
            (pg_hbm, pg_ref), (up_hbm, up_ref), (bytes_hbm, bytes_ref), (wk_hbm, wk_ref),
            (wv_hbm, wv_ref), (wq_hbm, wq_ref), (wo_hbm, wo_ref),
        ])
    ]
    for load in loads:
        load.start()

    starts = starts_ref[...].astype(F32)
    slot = lax.broadcasted_iota(jnp.int32, (slots, 1), 0)
    nth = lax.broadcasted_iota(jnp.int32, (slots, pcap), 1)
    lo = jnp.sum(jnp.where(nth == slot, starts, 0.0), axis=1, keepdims=True).astype(jnp.int32)
    lo = jnp.where(slot > pcap, byte_dev, lo)
    after = jnp.where(slot == pcap, 0, slot + 1)
    hi = jnp.sum(jnp.where(nth == after, starts, 0.0), axis=1, keepdims=True).astype(jnp.int32)
    hi = jnp.where((slot > pcap) | (slot == pcap - 1), byte_dev, hi)
    position = lax.broadcasted_iota(jnp.int32, (slots, byte_dev), 1)
    member = (position >= lo) & (position < hi)
    member_bf = jnp.where(member, 1.0, 0.0).astype(BF)
    mt_ref[...] = member_bf.T
    used = (slot < pcap) & (lo < byte_dev)
    owned = jnp.sum(jnp.where(used, 1.0, 0.0), axis=0, keepdims=True).astype(jnp.int32)
    is_prev = slot == pcap
    is_last = slot == owned - 1
    count_own = (hi - lo).astype(F32)
    base = jnp.where(lax.rem(s, 2) == 0, 0, rows_dev - owned)
    wanted = base + jnp.where(is_prev, -1, slot)

    def select(first, size):
        row = lax.broadcasted_iota(jnp.int32, (slots, size), 1) + first
        return jnp.where((row == wanted) & (used | is_prev), 1.0, 0.0).astype(BF)

    loads[0].wait()
    loads[1].wait()
    pg = pg_ref[...]

    def mix_partial(j):
        return dot(pg, up_ref[pl.ds(pl.multiple_of(j * cols, cols), cols), :], NT)

    for o in range(1, ntp):
        gm_send[o - 1] = mix_partial(tp_peer(o)).astype(BF)
    pl.semaphore_wait(barrier, len(peers))
    gm_copies = [
        send(gm_send.at[o - 1], gm_recv.at[o - 1], gm_ssem.at[o - 1], gm_rsem.at[o - 1], tp=tp_peer(o))
        for o in range(1, ntp)
    ]
    for copy in gm_copies:
        copy.start()
    gm_own = mix_partial(t)

    def exchange(src, dst, ssem, rsem):
        copies = [
            send(src.at[0], dst.at[0], ssem.at[0], rsem.at[0], seq=following),
            send(src.at[1], dst.at[1], ssem.at[1], rsem.at[1], seq=before),
        ]
        for copy in copies:
            copy.start()
        return copies

    loads[2].wait()
    pooled_sum = dot(member_bf, bytes_ref[...])
    count_row = jnp.broadcast_to(row_of(is_last, count_own), (1, width))
    a_send[0] = rows8(width, row_of(is_last, pooled_sum), count_row)
    count_row = jnp.broadcast_to(row_of(is_prev, count_own), (1, width))
    a_send[1] = rows8(width, row_of(is_prev, pooled_sum), count_row)
    a_copies = exchange(a_send, a_recv, a_ssem, a_rsem)

    loads[3].wait()
    k_ref[...] = dot(bytes_ref[...], wk_ref[...]).astype(BF)
    loads[4].wait()
    v_ref[...] = dot(bytes_ref[...], wv_ref[...]).astype(BF)

    for copy in gm_copies:
        copy.wait()
    total = gm_own
    for o in range(1, ntp):
        total = total + gm_recv[o - 1].astype(F32)
    mix_own[...] = total.astype(BF)
    m_copies = [
        send(mix_own.at[pl.ds(rows_dev - window, window)], mix_prev, m_ssem.at[0], m_rsem.at[0], seq=following),
        send(mix_own.at[pl.ds(0, window)], mix_next, m_ssem.at[1], m_rsem.at[1], seq=before),
    ]
    for copy in m_copies:
        copy.start()

    for copy in a_copies:
        copy.wait()
    lane = lax.broadcasted_iota(jnp.int32, (1, cols), 1)
    head0 = lane < HEAD

    def merged(own, received, index):
        width_here = own.shape[1]
        extra = jnp.where(is_prev, received[0, index:index + 1, 0:width_here], 0.0)
        return own + extra + jnp.where(is_last, received[1, index:index + 1, 0:width_here], 0.0)

    pooled_sum = merged(pooled_sum, a_recv, 0)
    counts = jnp.maximum(merged(count_own, a_recv, 1), 1.0)
    pooled_ref[...] = (pooled_sum / counts).astype(BF)
    loads[5].wait()
    queries = dot(pooled_ref[...], wq_ref[...]).astype(BF)

    for copy in m_copies:
        copy.wait()
    picked = dot(select(0, rows_dev), mix_own[...])
    picked = picked + dot(select(-window, window), mix_prev[...])
    picked = picked + dot(select(rows_dev, window), mix_next[...])
    mix_blk[...] = picked.astype(BF)
    mine = pl.ds(pl.multiple_of(t * cols, cols), cols)
    ag_copies = [
        send(mix_blk, mix_ref.at[:, mine], ag_ssem.at[o - 1], ag_rsem.at[o - 1], tp=tp_peer(o))
        for o in range(1, ntp)
    ]
    for copy in ag_copies:
        copy.start()
    mix_ref[:, mine] = mix_blk[...]

    def heads(value):
        zero = jnp.zeros_like(value)
        return jnp.concatenate([jnp.where(head0, value, zero), jnp.where(head0, zero, value)], axis=0)

    def unheads(value):
        return jnp.where(head0, value[:slots], value[slots:])

    member2 = jnp.concatenate([member, member], axis=0)
    queries2 = heads(queries)
    scores = jnp.where(member2, dot(queries2, k_ref[...], NT) * scale, NEG)
    peak = jnp.max(scores, axis=1, keepdims=True)
    expo = jnp.where(member2, jnp.exp(scores - peak), 0.0)
    sums = unheads(jnp.sum(expo, axis=1, keepdims=True))
    peaks = unheads(peak)
    partial_out = unheads(dot(expo.astype(BF), v_ref[...]))
    for i, mask in enumerate((is_last, is_prev)):
        b_send[i] = rows8(cols, row_of(mask, partial_out), row_of(mask, peaks), row_of(mask, sums))
    b_copies = exchange(b_send, b_recv, b_ssem, b_rsem)
    bytes_t[...] = bytes_ref[...].T
    pooled_t[...] = pooled_ref[...].T
    for copy in b_copies:
        copy.wait()

    def received(index, empty):
        other = jnp.where(is_last, b_recv[1, index:index + 1, :], empty)
        return jnp.where(is_prev, b_recv[0, index:index + 1, :], other)

    other_peaks = received(1, NEG)
    top = jnp.maximum(peaks, other_peaks)
    keep, add = jnp.exp(peaks - top), jnp.exp(other_peaks - top)
    denom = sums * keep + received(2, 0.0) * add
    denom = jnp.where(denom > 0.0, denom, 1.0)
    attended = ((partial_out * keep + received(0, 0.0) * add) / denom).astype(BF)
    factor = keep / denom
    factor2 = jnp.concatenate([factor[:, 0:1], factor[:, HEAD:HEAD + 1]], axis=0)
    weights = expo * factor2

    def stack(i, value):
        count = width // block
        stack_ref[pl.ds(i * count, count)] = value.astype(BF).reshape(count, block, cols)

    loads[6].wait()
    for copy in ag_copies:
        copy.wait()
    grad_attended = dot(mix_ref[...], wo_ref[...], NT).astype(BF)
    grad2 = heads(grad_attended)
    delta = jnp.sum(grad2.astype(F32) * heads(attended).astype(F32), axis=1, keepdims=True)
    grad_scores = (weights * (dot(grad2, v_ref[...], NT) - delta)).astype(BF)
    grad_queries = unheads(dot(grad_scores, k_ref[...])) * scale
    for i, mask in enumerate((is_last, is_prev)):
        d_send[i] = rows8(cols, row_of(mask, grad_queries))
    d_copies = exchange(d_send, d_recv, d_ssem, d_rsem)
    grad_keys = (dot(grad_scores, queries2, TN) * scale).astype(BF)
    grad_values = dot(weights.astype(BF), grad2, TN).astype(BF)
    stack(1, dot(bytes_t[...], grad_keys))
    stack(2, dot(bytes_t[...], grad_values))
    counted = jnp.where(is_prev, jnp.zeros_like(attended), attended)
    stack(3, dot(mix_ref[...], counted, TN))
    for copy in d_copies:
        copy.wait()
    grad_queries = merged(grad_queries, d_recv, 0).astype(BF)
    counted = jnp.where(is_prev, jnp.zeros_like(grad_queries), grad_queries)
    stack(0, dot(pooled_t[...], counted))

    per = block * nz // chunks
    for i, o in enumerate(order):
        target = lax.rem(z + o, nz) * NY

        def reorder(q, _, i=i, target=target):
            y_send[q, pl.ds(i * block, block), :] = stack_ref[slots_ref[target + q]]
            return 0

        lax.fori_loop(0, NY, reorder, 0)
    y_copies = []
    for c in range(chunks):
        part = pl.ds(c * per, per)
        y_copies.append([
            send(
                y_send.at[lax.rem(y + o, NY), part], y_recv.at[o - 1, part],
                y_ssem.at[o - 1, c], y_rsem.at[o - 1, c], seq=y_peer(o),
            )
            for o in range(1, NY)
        ])
        for copy in y_copies[-1]:
            copy.start()

    pb_ref[...] = (dot(grad_queries, wq_ref[...], NT) / counts).astype(BF)

    def byte_partial(j):
        columns = pl.ds(pl.multiple_of(j * cols, cols), cols)
        value = dot(grad_keys, wk_ref[columns, :], NT) + dot(grad_values, wv_ref[columns, :], NT)
        return value + dot(mt_ref[...], pb_ref[:, columns])

    p_copies = []
    for o in range(1, ntp):
        part_send[o - 1] = byte_partial(tp_peer(o)).astype(BF)
        p_copies.append(send(
            part_send.at[o - 1], part_recv.at[o - 1], p_ssem.at[o - 1], p_rsem.at[o - 1], tp=tp_peer(o),
        ))
        p_copies[-1].start()
    mix_mean = (mix_blk[...].astype(F32) / counts).astype(BF)
    part_own[...] = byte_partial(t) + dot(mt_ref[...], mix_mean)

    z_copies = []
    for c in range(chunks):
        for copy in y_copies[c]:
            copy.wait()
        part = pl.ds(c * per, per)
        summed = y_send[y, part, :].astype(F32)
        for o in range(1, NY):
            summed = summed + y_recv[o - 1, part, :].astype(F32)
        z_send[part, :] = summed.astype(BF)
        for i in range(c * nz // chunks, (c + 1) * nz // chunks):
            if order[i]:
                z_copies.append(send(
                    z_send.at[pl.ds(i * block, block)], z_recv.at[i], z_ssem.at[i], z_rsem.at[i],
                    seq=z_peer(order[i]),
                ))
                z_copies[-1].start()

    total = part_own[...]
    for o in range(1, ntp):
        p_copies[o - 1].wait()
        total = total + part_recv[o - 1].astype(F32)
    byte_out[...] = total.astype(BF)

    total = z_send[pl.ds((nz - 1) * block, block), :].astype(F32)
    for i, copy in enumerate(z_copies):
        copy.wait()
        total = total + z_recv[i].astype(F32)
    owned_out[...] = total


def local(
    byte_states, patch_starts, query_weight, key_weight, value_weight, out_weight, up_weight, patch_grad,
    owner_slots, *, n_seq, ntp,
):
    byte_dev, width = byte_states.shape
    pcap = patch_starts.shape[0]
    rows_dev, features = patch_grad.shape
    cols = query_weight.shape[1]
    slots = up16(pcap + 1)
    window = up16(pcap - rows_dev + 1)
    nz = n_seq // NY
    chunks = 4 if nz % 4 == 0 else nz
    block = 4 * width // n_seq
    vmem = pl.BlockSpec(memory_space=pltpu.VMEM)
    hbm = pl.BlockSpec(memory_space=pltpu.HBM)
    dma = pltpu.SemaphoreType.DMA
    pairs = [dma((2,))] * 2
    return pl.pallas_call(
        functools.partial(kernel, (n_seq, ntp, pcap, rows_dev, window, chunks)),
        out_shape=(
            jax.ShapeDtypeStruct((byte_dev, cols), BF),
            jax.ShapeDtypeStruct((block, cols), F32),
        ),
        in_specs=[vmem, pl.BlockSpec(memory_space=pltpu.SMEM)] + [hbm] * 7,
        out_specs=(vmem, vmem),
        scratch_shapes=[
            pltpu.VMEM((byte_dev, width), BF),
            pltpu.VMEM((width, cols), BF),
            pltpu.VMEM((width, cols), BF),
            pltpu.VMEM((width, cols), BF),
            pltpu.VMEM((cols, width), BF),
            pltpu.VMEM((width, features), BF),
            pltpu.VMEM((rows_dev, features), BF),
            pltpu.VMEM((width, byte_dev), BF),
            pltpu.VMEM((byte_dev, cols), BF),
            pltpu.VMEM((byte_dev, cols), BF),
            pltpu.VMEM((slots, width), BF),
            pltpu.VMEM((width, slots), BF),
            pltpu.VMEM((byte_dev, slots), BF),
            pltpu.VMEM((slots, width), BF),
            pltpu.VMEM((slots, width), BF),
            pltpu.VMEM((n_seq, block, cols), BF),
            pltpu.VMEM((ntp - 1, rows_dev, cols), BF),
            pltpu.VMEM((ntp - 1, rows_dev, cols), BF),
            pltpu.VMEM((rows_dev, cols), BF),
            pltpu.VMEM((window, cols), BF),
            pltpu.VMEM((window, cols), BF),
            pltpu.VMEM((slots, cols), BF),
            pltpu.VMEM((2, 8, width), F32),
            pltpu.VMEM((2, 8, width), F32),
            pltpu.VMEM((2, 8, cols), F32),
            pltpu.VMEM((2, 8, cols), F32),
            pltpu.VMEM((2, 8, cols), F32),
            pltpu.VMEM((2, 8, cols), F32),
            pltpu.VMEM((ntp - 1, byte_dev, cols), BF),
            pltpu.VMEM((ntp - 1, byte_dev, cols), BF),
            pltpu.VMEM((byte_dev, cols), F32),
            pltpu.VMEM((NY, nz * block, cols), BF),
            pltpu.VMEM((NY - 1, nz * block, cols), BF),
            pltpu.VMEM((nz * block, cols), BF),
            pltpu.VMEM((nz - 1, block, cols), BF),
            dma((7,)),
            dma((ntp - 1,)), dma((ntp - 1,)),
            *pairs,
            dma((ntp - 1,)), dma((ntp - 1,)),
            *pairs, *pairs, *pairs,
            dma((ntp - 1,)), dma((ntp - 1,)),
            dma((NY - 1, chunks)), dma((NY - 1, chunks)),
            dma((nz - 1,)), dma((nz - 1,)),
        ],
        compiler_params=pltpu.CompilerParams(
            collective_id=0, has_side_effects=True, vmem_limit_bytes=62 * 1024 * 1024
        ),
    )(
        patch_starts.reshape(1, pcap), owner_slots, byte_states, query_weight, key_weight, value_weight,
        out_weight, up_weight, patch_grad,
    )


def solution(mesh):
    in_specs = (
        P("seq", None),
        P("seq"),
        P(None, "tp"),
        P(None, "tp"),
        P(None, "tp"),
        P("tp", None),
        P(None, "tp"),
        P("seq", "tp"),
        P(),
    )
    out_specs = (P("seq", "tp"), P("seq", "tp"))
    step = functools.partial(local, n_seq=mesh.shape["seq"], ntp=mesh.shape["tp"])
    return jax.shard_map(step, mesh=mesh, in_specs=in_specs, out_specs=out_specs, check_vma=False)
```

```python
import functools

import jax
import jax.numpy as jnp
from jax import lax
from jax.experimental import pallas as pl
from jax.experimental.pallas import tpu as pltpu
from jax.sharding import PartitionSpec as P

HEAD = 64
NY = 4
NEG = -1e30
F32 = jnp.float32
BF = jnp.bfloat16
NT = (((1,), (1,)), ((), ()))
TN = (((0,), (0,)), ((), ()))


def dot(a, b, dims=(((1,), (0,)), ((), ()))):
    return lax.dot_general(a, b, dims, preferred_element_type=F32)


def up16(n):
    return -(-n // 16) * 16


def row_of(mask, value):
    return jnp.sum(jnp.where(mask, value, 0.0), axis=0, keepdims=True)


def rows8(width, *rows):
    index = lax.broadcasted_iota(jnp.int32, (8, width), 0)
    out = jnp.zeros((8, width), F32)
    for i, row in enumerate(rows):
        out = jnp.where(index == i, row, out)
    return out


def z_chunks(nz):
    if nz == 16:
        return [[8, 7, -7], [6, -6, 5, -5], [4, -4, 3, -3], [2, -2, 1, -1, 0]]
    return [[2], [1, -1], [0]]


def x_order(nx):
    return sorted(range(1, nx), key=lambda d: -min(d, nx - d)) + [0]


def kernel(
    sizes,
    starts_ref, slots_ref, bytes_hbm, wq_hbm, wk_hbm, wv_hbm, wo_hbm, up_hbm, pg_hbm,
    byte_out, owned_out,
    bytes_ref, wq_ref, wk_ref, wv_ref, wo_ref, up_ref, pg_ref,
    bytes_t, k_ref, v_ref, gk_ref, gv_ref, pooled_ref, pooled_t, mt_ref, mix_ref, pb_ref, stack_ref,
    gm_first, gm_send, gm_recv, mix_own, mix_buf,
    a_send, a_recv, b_send, b_recv,
    part, mate_recv, px_send, px_recv, y_send, y_far, y_dir, z_send, zf_recv, z_recv,
    load_sem, gm_ssem, gm_rsem, ag_ssem, ag_rsem, a_ssem, a_rsem, b_ssem, b_rsem,
    p_ssem, p_rsem, px_ssem, px_rsem, y_ssem, y_rsem, zf_ssem, zf_rsem, z_ssem, z_rsem,
):
    n_seq, ntp, pcap, rows_dev, window = sizes
    nz, nx = n_seq // NY, ntp // 2
    reach = nz // 4
    slots = mt_ref.shape[1]
    byte_dev, width = bytes_ref.shape
    cols = k_ref.shape[1]
    block = owned_out.shape[0]
    scale = HEAD ** -0.5
    s = lax.axis_index("seq")
    t = lax.axis_index("tp")
    y, z = lax.rem(s, NY), s // NY
    x, core = t // 2, lax.rem(t, 2)
    odd = lax.rem(s, 2)
    following, before = lax.rem(s + 1, n_seq), lax.rem(s + n_seq - 1, n_seq)
    partner = s + 1 - 2 * odd
    plus, minus = z * NY + lax.rem(y + 1, NY), z * NY + lax.rem(y + NY - 1, NY)
    chunks = z_chunks(nz)
    order = [o for chunk in chunks for o in chunk]
    near = [o for o in order if 0 < abs(o) <= reach]
    far = [o for o in order if abs(o) > reach]
    mine = pl.ds(pl.multiple_of(t * cols, cols), cols)
    my_half = pl.ds(pl.multiple_of(core * cols, cols), cols)
    mate_half = pl.ds(pl.multiple_of((1 - core) * cols, cols), cols)
    everyone = [(o, d) for o in x_order(nx) for d in (0, 1)]
    others = [pair for pair in everyone if pair != (0, 0)]

    def tp_peer(o, d):
        return 2 * lax.rem(x + o, nx) + lax.rem(core + d, 2)

    def z_peer(o):
        return lax.rem(z + o + nz, nz) * NY + y

    def send(src, dst, ssem, rsem, **where):
        return pltpu.make_async_remote_copy(
            src_ref=src, dst_ref=dst, send_sem=ssem, recv_sem=rsem,
            device_id=where, device_id_type=pl.DeviceIdType.MESH,
        )

    loads = [
        pltpu.make_async_copy(src, dst, load_sem.at[i])
        for i, (src, dst) in enumerate([
            (pg_hbm, pg_ref), (up_hbm, up_ref), (bytes_hbm, bytes_ref), (wk_hbm, wk_ref),
            (wv_hbm, wv_ref), (wq_hbm, wq_ref), (wo_hbm, wo_ref),
        ])
    ]
    for load in loads:
        load.start()

    barrier = pltpu.get_barrier_semaphore()
    peers = [{"tp": tp_peer(o, d)} for o, d in others]
    peers += [{"seq": partner, "tp": tp_peer(o, d)} for o, d in everyone]
    peers += [{"seq": before, "tp": tp_peer(o, d)} for o, d in everyone]
    peers += [{"seq": following}, {"seq": plus}, {"seq": minus}]
    peers += [{"seq": z_peer(o)} for o in near]
    for peer in peers:
        pl.semaphore_signal(barrier, inc=1, device_id=peer, device_id_type=pl.DeviceIdType.MESH)

    loads[0].wait()
    loads[1].wait()
    for o in x_order(nx):
        rows = pl.ds(pl.multiple_of(lax.rem(x + o, nx) * 2 * cols, 2 * cols), 2 * cols)
        value = dot(pg_ref[...], up_ref[rows, :], NT)
        if o == 0:
            gm_first[...] = value
        gm_send[o] = value.astype(BF)
    pl.semaphore_wait(barrier, len(peers))
    gm_copies = []
    for k, (o, d) in enumerate(others):
        half = mate_half if d else my_half
        gm_copies.append(send(gm_send.at[o, :, half], gm_recv.at[k], gm_ssem.at[k], gm_rsem.at[k], tp=tp_peer(o, d)))
        gm_copies[-1].start()

    starts = starts_ref[...].astype(F32)
    slot = lax.broadcasted_iota(jnp.int32, (slots, 1), 0)
    nth = lax.broadcasted_iota(jnp.int32, (slots, pcap), 1)
    lo = jnp.sum(jnp.where(nth == slot, starts, 0.0), axis=1, keepdims=True).astype(jnp.int32)
    lo = jnp.where(slot > pcap, byte_dev, lo)
    after = jnp.where(slot == pcap, 0, slot + 1)
    hi = jnp.sum(jnp.where(nth == after, starts, 0.0), axis=1, keepdims=True).astype(jnp.int32)
    hi = jnp.where((slot > pcap) | (slot == pcap - 1), byte_dev, hi)
    position = lax.broadcasted_iota(jnp.int32, (slots, byte_dev), 1)
    member = (position >= lo) & (position < hi)
    member_bf = jnp.where(member, 1.0, 0.0).astype(BF)
    mt_ref[...] = member_bf.T
    used = (slot < pcap) & (lo < byte_dev)
    owned = jnp.sum(jnp.where(used, 1.0, 0.0), axis=0, keepdims=True).astype(jnp.int32)
    is_prev = slot == pcap
    is_last = slot == owned - 1
    count_own = (hi - lo).astype(F32)

    def exchange(src, dst, ssem, rsem):
        copies = [
            send(src.at[0], dst.at[0], ssem.at[0], rsem.at[0], seq=following),
            send(src.at[1], dst.at[1], ssem.at[1], rsem.at[1], seq=before),
        ]
        for copy in copies:
            copy.start()
        return copies

    loads[2].wait()
    pooled_sum = dot(member_bf, bytes_ref[...])
    for i, mask in enumerate((is_last, is_prev)):
        count_row = jnp.broadcast_to(row_of(mask, count_own), (1, width))
        a_send[i] = rows8(width, row_of(mask, pooled_sum), count_row)
    a_copies = exchange(a_send, a_recv, a_ssem, a_rsem)

    loads[3].wait()
    k_ref[...] = dot(bytes_ref[...], wk_ref[...]).astype(BF)
    loads[4].wait()
    v_ref[...] = dot(bytes_ref[...], wv_ref[...]).astype(BF)

    for copy in gm_copies:
        copy.wait()
    total = gm_first[:, my_half]
    for k in range(len(others)):
        total = total + gm_recv[k].astype(F32)
    mix_own[...] = total.astype(BF)
    shared = pl.ds(pl.multiple_of((rows_dev - window) * (1 - odd), 16), window)
    ag_copies = []
    for k, (o, d) in enumerate(everyone):
        routes = [
            (mix_own.at[shared], pl.ds(rows_dev, window), partner),
            (mix_own.at[pl.ds(rows_dev - 16, 16)], pl.ds(rows_dev + window, 16), following),
        ]
        if (o, d) != (0, 0):
            routes.append((mix_own, pl.ds(0, rows_dev), s))
        for i, (src, rows, seq) in enumerate(routes):
            ag_copies.append(send(
                src, mix_buf.at[rows, mine], ag_ssem.at[i, k], ag_rsem.at[i, k], seq=seq, tp=tp_peer(o, d),
            ))
            ag_copies[-1].start()
    mix_buf[pl.ds(0, rows_dev), mine] = mix_own[...]

    for copy in a_copies:
        copy.wait()
    lane = lax.broadcasted_iota(jnp.int32, (1, cols), 1)
    head0 = lane < HEAD

    def merged(own, received, index):
        width_here = own.shape[1]
        extra = jnp.where(is_prev, received[0, index:index + 1, 0:width_here], 0.0)
        return own + extra + jnp.where(is_last, received[1, index:index + 1, 0:width_here], 0.0)

    pooled_sum = merged(pooled_sum, a_recv, 0)
    counts = jnp.maximum(merged(count_own, a_recv, 1), 1.0)
    pooled_ref[...] = (pooled_sum / counts).astype(BF)
    loads[5].wait()
    queries = dot(pooled_ref[...], wq_ref[...]).astype(BF)

    def heads(value):
        zero = jnp.zeros_like(value)
        return jnp.concatenate([jnp.where(head0, value, zero), jnp.where(head0, zero, value)], axis=0)

    def unheads(value):
        half = value.shape[0] // 2
        return jnp.where(head0, value[:half], value[half:])

    member2 = jnp.concatenate([member, member], axis=0)
    queries2 = heads(queries)
    scores = jnp.where(member2, dot(queries2, k_ref[...], NT) * scale, NEG)
    peak = jnp.max(scores, axis=1, keepdims=True)
    expo = jnp.where(member2, jnp.exp(scores - peak), 0.0)
    expo_bf = expo.astype(BF)
    sums = unheads(jnp.sum(expo, axis=1, keepdims=True))
    peaks = unheads(peak)
    partial_out = unheads(dot(expo_bf, v_ref[...]))
    partial_keys = unheads(dot(expo_bf, k_ref[...]))
    chosen = [
        heads(jnp.broadcast_to(jnp.where(mask, 1.0, 0.0), (slots, cols)).astype(BF)) for mask in (is_last, is_prev)
    ]
    spread = dot(expo_bf, jnp.concatenate(chosen, axis=1), TN)
    values = v_ref[...].astype(F32)
    spread = (spread * jnp.concatenate([values, values], axis=1)).astype(BF)
    products = dot(spread, k_ref[...], TN)
    for i, mask in enumerate((is_last, is_prev)):
        b_send[i, 0:8, :] = rows8(
            cols, row_of(mask, partial_out), row_of(mask, peaks), row_of(mask, sums), row_of(mask, partial_keys),
        )
        b_send[i, 8:8 + HEAD, :] = unheads(products[i * cols:(i + 1) * cols])
    b_copies = exchange(b_send, b_recv, b_ssem, b_rsem)
    bytes_t[...] = bytes_ref[...].T
    pooled_t[...] = pooled_ref[...].T
    for copy in b_copies:
        copy.wait()

    def received(index, empty):
        other = jnp.where(is_last, b_recv[1, index:index + 1, :], empty)
        return jnp.where(is_prev, b_recv[0, index:index + 1, :], other)

    other_peaks = received(1, NEG)
    top = jnp.maximum(peaks, other_peaks)
    keep, add = jnp.exp(peaks - top), jnp.exp(other_peaks - top)
    denom = sums * keep + received(2, 0.0) * add
    denom = jnp.where(denom > 0.0, denom, 1.0)
    attended = ((partial_out * keep + received(0, 0.0) * add) / denom).astype(BF)
    attended2 = heads(attended).astype(F32)
    factor = keep / denom
    factor2 = jnp.concatenate([factor[:, 0:1], factor[:, HEAD:HEAD + 1]], axis=0)
    weights = expo * factor2
    other_factor = add / denom
    base = jnp.where(odd == 0, 0, rows_dev - owned)
    wanted = base + jnp.where(is_prev, -1, slot)
    row = lax.broadcasted_iota(jnp.int32, (slots, rows_dev + window + 16), 1)
    place = jnp.where(row < rows_dev, row, row - odd * (rows_dev + window))
    place = jnp.where(row < rows_dev + window, place, row - (rows_dev + window + 16) - odd * (2 * byte_dev))
    select = jnp.where((place == wanted) & (used | is_prev), 1.0, 0.0).astype(BF)

    def stack(i, value):
        count = width // block
        stack_ref[pl.ds(i * count, count)] = value.astype(BF).reshape(count, block, cols)

    loads[6].wait()
    for copy in ag_copies:
        copy.wait()
    mix_ref[...] = dot(select, mix_buf[...]).astype(BF)
    grad_attended = dot(mix_ref[...], wo_ref[...], NT).astype(BF)
    grad2 = heads(grad_attended)
    delta = jnp.sum(grad2.astype(F32) * attended2, axis=1, keepdims=True)
    grad_scores = (weights * (dot(grad2, v_ref[...], NT) - delta)).astype(BF)
    grad_queries = unheads(dot(grad_scores, k_ref[...]))
    delta = unheads(delta)
    nth = lax.broadcasted_iota(jnp.int32, (HEAD, cols), 0)
    for mask, i in ((is_prev, 0), (is_last, 1)):
        row = row_of(mask, grad_attended.astype(F32))
        column0 = jnp.sum(jnp.where(lane == nth, row, 0.0), axis=1, keepdims=True)
        column1 = jnp.sum(jnp.where(lane == nth + HEAD, row, 0.0), axis=1, keepdims=True)
        whole = jnp.sum(jnp.where(head0, column0, column1) * b_recv[i, 8:8 + HEAD, :], axis=0, keepdims=True)
        whole = whole - row_of(mask, delta) * b_recv[i, 3:4, :]
        grad_queries = grad_queries + jnp.where(mask, row_of(mask, other_factor) * whole, 0.0)
    grad_queries = (grad_queries * scale).astype(BF)
    gk_ref[...] = (dot(grad_scores, queries2, TN) * scale).astype(BF)
    gv_ref[...] = dot(weights.astype(BF), grad2, TN).astype(BF)
    stack(1, dot(bytes_t[...], gk_ref[...]))
    stack(2, dot(bytes_t[...], gv_ref[...]))
    stack(3, dot(mix_ref[...], jnp.where(is_prev, jnp.zeros_like(attended), attended), TN))
    stack(0, dot(pooled_t[...], jnp.where(is_prev, jnp.zeros_like(grad_queries), grad_queries)))

    begins = [sum(len(chunk) for chunk in chunks[:c]) * block for c in range(len(chunks) + 1)]
    opposite, above, below = lax.rem(y + 2, NY), lax.rem(y + 1, NY), lax.rem(y + 3, NY)
    y_copies = {}

    def y_send_to(c, i, src, dst, seq):
        y_copies[c, i] = send(src, dst, y_ssem.at[c, i], y_rsem.at[c, i], seq=seq)
        y_copies[c, i].start()

    def halves(c):
        half = (begins[c + 1] - begins[c]) // 2
        return pl.ds(begins[c], half), pl.ds(begins[c] + half, half)

    def y_first(c):
        for i in range(begins[c] // block, begins[c + 1] // block):
            target = lax.rem(z + order[i] + nz, nz) * NY

            def reorder(q, _, i=i, target=target):
                y_send[q, pl.ds(i * block, block), :] = stack_ref[slots_ref[target + q]]
                return 0

            lax.fori_loop(0, NY, reorder, 0)
        one, two = halves(c)
        y_send_to(c, 0, y_send.at[opposite, one], y_far.at[0, one], plus)
        y_send_to(c, 1, y_send.at[opposite, two], y_far.at[1, two], minus)
        y_send_to(c, 2, y_send.at[above, two], y_dir.at[0, two], plus)
        y_send_to(c, 3, y_send.at[below, one], y_dir.at[1, one], minus)

    def y_second(c):
        one, two = halves(c)
        for i, (rows, q, seq) in enumerate([(one, above, plus), (two, below, minus)]):
            y_copies[c, i].wait_recv()
            value = y_send[q, rows, :].astype(F32) + y_far[i, rows, :].astype(F32)
            y_send[q, rows, :] = value.astype(BF)
            y_send_to(c, 4 + i, y_send.at[q, rows], y_dir.at[i, rows], seq)

    z_copies, far_copies = {}, {}

    def z_rows(o):
        return pl.ds(order.index(o) * block, block)

    def y_sum(c):
        for i in (2, 3, 4, 5):
            y_copies[c, i].wait_recv()
        rows = pl.ds(begins[c], begins[c + 1] - begins[c])
        value = y_send[y, rows, :].astype(F32) + y_dir[0, rows, :].astype(F32) + y_dir[1, rows, :].astype(F32)
        z_send[rows, :] = value.astype(BF)
        for o in chunks[c]:
            if abs(o) > reach:
                i = far.index(o)
                step = o - reach if o > 0 else o + reach
                far_copies[o] = send(
                    z_send.at[z_rows(o)], zf_recv.at[i], zf_ssem.at[i], zf_rsem.at[i], seq=z_peer(step),
                )
                far_copies[o].start()
        for o in sorted((o for o in chunks[c] if 0 < abs(o) <= reach), key=abs):
            if abs(o) == reach:
                value = z_send[z_rows(o), :].astype(F32)
                for i, source in enumerate(far):
                    if (source > 0) == (o > 0):
                        far_copies[source].wait_recv()
                        value = value + zf_recv[i].astype(F32)
                z_send[z_rows(o), :] = value.astype(BF)
            i = near.index(o)
            z_copies[o] = send(z_send.at[z_rows(o)], z_recv.at[i], z_ssem.at[i], z_rsem.at[i], seq=z_peer(o))
            z_copies[o].start()

    p_copies, px_copies = {}, {}

    def p_block(o):
        columns = pl.ds(pl.multiple_of(lax.rem(x + o, nx) * 2 * cols, 2 * cols), 2 * cols)
        value = dot(gk_ref[...], wk_ref[columns, :], NT) + dot(gv_ref[...], wv_ref[columns, :], NT)
        part[o] = (value + dot(mt_ref[...], pb_ref[:, columns])).astype(BF)
        p_copies[o] = send(
            part.at[o, :, mate_half], mate_recv.at[o], p_ssem.at[o], p_rsem.at[o], tp=tp_peer(0, 1),
        )
        p_copies[o].start()

    def p_pair(o):
        p_copies[o].wait_recv()
        return part[o, :, my_half].astype(F32) + mate_recv[o].astype(F32)

    def p_x(o):
        px_send[o - 1] = p_pair(o).astype(BF)
        px_copies[o] = send(
            px_send.at[o - 1], px_recv.at[o - 1], px_ssem.at[o - 1], px_rsem.at[o - 1], tp=tp_peer(o, 0),
        )
        px_copies[o].start()

    y_first(0)
    y_first(1)
    pb_ref[...] = (dot(grad_queries, wq_ref[...], NT) / counts).astype(BF)
    for step in range(max(nx, len(chunks)) + 1):
        if step < nx:
            p_block(x_order(nx)[step])
        if 0 <= step - 2 < len(chunks):
            y_sum(step - 2)
        if step < len(chunks):
            y_second(step)
        if step + 2 < len(chunks):
            y_first(step + 2)
        if 0 < step < nx:
            p_x(x_order(nx)[step - 1])
    for c in range(max(nx, len(chunks)) - 1, len(chunks)):
        y_sum(c)

    mix_mean = (mix_ref[:, mine].astype(F32) / counts).astype(BF)
    total = p_pair(0) + dot(mt_ref[...], mix_mean)
    for o in px_copies:
        px_copies[o].wait_recv()
        total = total + px_recv[o - 1].astype(F32)
    byte_out[...] = total.astype(BF)

    total = z_send[z_rows(0), :].astype(F32)
    for i, o in enumerate(near):
        z_copies[o].wait_recv()
        total = total + z_recv[i].astype(F32)
    owned_out[...] = total
    for copies in (p_copies, px_copies, y_copies, far_copies, z_copies):
        for copy in copies.values():
            copy.wait_send()


def local(
    byte_states, patch_starts, query_weight, key_weight, value_weight, out_weight, up_weight, patch_grad,
    owner_slots, *, n_seq, ntp,
):
    byte_dev, width = byte_states.shape
    pcap = patch_starts.shape[0]
    rows_dev, features = patch_grad.shape
    cols = query_weight.shape[1]
    slots = up16(pcap + 1)
    window = up16(pcap - rows_dev + 1)
    nz, nx = n_seq // NY, ntp // 2
    order = [o for chunk in z_chunks(nz) for o in chunk]
    near = sum(0 < abs(o) <= nz // 4 for o in order)
    far = nz - 1 - near
    block = 4 * width // n_seq
    vmem = pl.BlockSpec(memory_space=pltpu.VMEM)
    hbm = pl.BlockSpec(memory_space=pltpu.HBM)
    dma = pltpu.SemaphoreType.DMA
    return pl.pallas_call(
        functools.partial(kernel, (n_seq, ntp, pcap, rows_dev, window)),
        out_shape=(
            jax.ShapeDtypeStruct((byte_dev, cols), BF),
            jax.ShapeDtypeStruct((block, cols), F32),
        ),
        in_specs=[vmem, pl.BlockSpec(memory_space=pltpu.SMEM)] + [hbm] * 7,
        out_specs=(vmem, vmem),
        scratch_shapes=[
            pltpu.VMEM((byte_dev, width), BF),
            pltpu.VMEM((width, cols), BF),
            pltpu.VMEM((width, cols), BF),
            pltpu.VMEM((width, cols), BF),
            pltpu.VMEM((cols, width), BF),
            pltpu.VMEM((width, features), BF),
            pltpu.VMEM((rows_dev, features), BF),
            pltpu.VMEM((width, byte_dev), BF),
            pltpu.VMEM((byte_dev, cols), BF),
            pltpu.VMEM((byte_dev, cols), BF),
            pltpu.VMEM((byte_dev, cols), BF),
            pltpu.VMEM((byte_dev, cols), BF),
            pltpu.VMEM((slots, width), BF),
            pltpu.VMEM((width, slots), BF),
            pltpu.VMEM((byte_dev, slots), BF),
            pltpu.VMEM((slots, width), BF),
            pltpu.VMEM((slots, width), BF),
            pltpu.VMEM((n_seq, block, cols), BF),
            pltpu.VMEM((rows_dev, 2 * cols), F32),
            pltpu.VMEM((nx, rows_dev, 2 * cols), BF),
            pltpu.VMEM((ntp - 1, rows_dev, cols), BF),
            pltpu.VMEM((rows_dev, cols), BF),
            pltpu.VMEM((rows_dev + window + 16, width), BF),
            pltpu.VMEM((2, 8, width), F32),
            pltpu.VMEM((2, 8, width), F32),
            pltpu.VMEM((2, 8 + HEAD, cols), F32),
            pltpu.VMEM((2, 8 + HEAD, cols), F32),
            pltpu.VMEM((nx, byte_dev, 2 * cols), BF),
            pltpu.VMEM((nx, byte_dev, cols), BF),
            pltpu.VMEM((nx - 1, byte_dev, cols), BF),
            pltpu.VMEM((nx - 1, byte_dev, cols), BF),
            pltpu.VMEM((NY, nz * block, cols), BF),
            pltpu.VMEM((2, nz * block, cols), BF),
            pltpu.VMEM((2, nz * block, cols), BF),
            pltpu.VMEM((nz * block, cols), BF),
            pltpu.VMEM((far, block, cols), BF),
            pltpu.VMEM((near, block, cols), BF),
            dma((7,)),
            dma((ntp - 1,)), dma((ntp - 1,)),
            dma((3, ntp)), dma((3, ntp)),
            dma((2,)), dma((2,)),
            dma((2,)), dma((2,)),
            dma((nx,)), dma((nx,)),
            dma((nx - 1,)), dma((nx - 1,)),
            dma((4, 6)), dma((4, 6)),
            dma((far,)), dma((far,)),
            dma((near,)), dma((near,)),
        ],
        compiler_params=pltpu.CompilerParams(
            collective_id=0, has_side_effects=True, vmem_limit_bytes=62 * 1024 * 1024
        ),
    )(
        patch_starts.reshape(1, pcap), owner_slots, byte_states, query_weight, key_weight, value_weight,
        out_weight, up_weight, patch_grad,
    )


def solution(mesh):
    in_specs = (
        P("seq", None),
        P("seq"),
        P(None, "tp"),
        P(None, "tp"),
        P(None, "tp"),
        P("tp", None),
        P(None, "tp"),
        P("seq", "tp"),
        P(),
    )
    out_specs = (P("seq", "tp"), P("seq", "tp"))
    step = functools.partial(local, n_seq=mesh.shape["seq"], ntp=mesh.shape["tp"])
    return jax.shard_map(step, mesh=mesh, in_specs=in_specs, out_specs=out_specs, check_vma=False)
```

```python
import functools

import jax
import jax.numpy as jnp
from jax import lax
from jax.experimental import pallas as pl
from jax.experimental.pallas import tpu as pltpu
from jax.sharding import PartitionSpec as P

HEAD = 64
NY = 4
NEG = -1e30
F32 = jnp.float32
BF = jnp.bfloat16
NT = (((1,), (1,)), ((), ()))
TN = (((0,), (0,)), ((), ()))


def dot(a, b, dims=(((1,), (0,)), ((), ()))):
    return lax.dot_general(a, b, dims, preferred_element_type=F32)


def up16(n):
    return -(-n // 16) * 16


def row_of(mask, value):
    return jnp.sum(jnp.where(mask, value, 0.0), axis=0, keepdims=True)


def rows8(width, *rows):
    index = lax.broadcasted_iota(jnp.int32, (8, width), 0)
    out = jnp.zeros((8, width), F32)
    for i, row in enumerate(rows):
        out = jnp.where(index == i, row, out)
    return out


def z_chunks(nz):
    if nz == 16:
        return [[8, 7, -7], [6, -6, 5, -5], [4, -4, 3, -3], [2, -2, 1, -1, 0]]
    return [[2], [1, -1], [0]]


def x_order(nx):
    return sorted(range(1, nx), key=lambda d: -min(d, nx - d)) + [0]


def kernel(
    sizes,
    starts_hbm, slots_hbm, bytes_hbm, wq_hbm, wk_hbm, wv_hbm, wo_hbm, up_hbm, pg_hbm,
    byte_out, owned_out,
    starts_ref, slots_ref, bytes_ref, wq_ref, wk_ref, wv_ref, wo_ref, up_ref, pg_ref,
    bytes_t, k_ref, v_ref, gk_ref, gv_ref, pooled_ref, pooled_t, mt_ref, mix_ref, pb_ref, stack_ref,
    gm_first, gm_send, gm_recv, mix_own, mix_buf,
    a_send, a_recv, b_send, b_recv,
    part, mate_recv, px_send, px_recv, y_send, y_far, y_dir, z_send, zf_recv, z_recv,
    load_sem, gm_ssem, gm_rsem, ag_ssem, ag_rsem, a_ssem, a_rsem, b_ssem, b_rsem,
    p_ssem, p_rsem, px_ssem, px_rsem, y_ssem, y_rsem, zf_ssem, zf_rsem, z_ssem, z_rsem,
):
    n_seq, ntp, pcap, rows_dev, window = sizes
    nz, nx = n_seq // NY, ntp // 2
    reach = nz // 4
    slots = mt_ref.shape[1]
    byte_dev, width = bytes_ref.shape
    cols = k_ref.shape[1]
    block = owned_out.shape[0]
    scale = HEAD ** -0.5
    s = lax.axis_index("seq")
    t = lax.axis_index("tp")
    y, z = lax.rem(s, NY), s // NY
    x, core = t // 2, lax.rem(t, 2)
    odd = lax.rem(s, 2)
    following, before = lax.rem(s + 1, n_seq), lax.rem(s + n_seq - 1, n_seq)
    partner = s + 1 - 2 * odd
    plus, minus = z * NY + lax.rem(y + 1, NY), z * NY + lax.rem(y + NY - 1, NY)
    chunks = z_chunks(nz)
    order = [o for chunk in chunks for o in chunk]
    near = [o for o in order if 0 < abs(o) <= reach]
    far = [o for o in order if abs(o) > reach]
    mine = pl.ds(pl.multiple_of(t * cols, cols), cols)
    my_half = pl.ds(pl.multiple_of(core * cols, cols), cols)
    mate_half = pl.ds(pl.multiple_of((1 - core) * cols, cols), cols)
    everyone = [(o, d) for o in x_order(nx) for d in (0, 1)]
    others = [pair for pair in everyone if pair != (0, 0)]

    def tp_peer(o, d):
        return 2 * lax.rem(x + o, nx) + lax.rem(core + d, 2)

    def z_peer(o):
        return lax.rem(z + o + nz, nz) * NY + y

    def send(src, dst, ssem, rsem, **where):
        return pltpu.make_async_remote_copy(
            src_ref=src, dst_ref=dst, send_sem=ssem, recv_sem=rsem,
            device_id=where, device_id_type=pl.DeviceIdType.MESH,
        )

    loads = [
        pltpu.make_async_copy(src, dst, load_sem.at[i])
        for i, (src, dst) in enumerate([
            (pg_hbm, pg_ref), (up_hbm, up_ref), (bytes_hbm, bytes_ref), (wk_hbm, wk_ref),
            (wv_hbm, wv_ref), (wq_hbm, wq_ref), (wo_hbm, wo_ref), (starts_hbm, starts_ref), (slots_hbm, slots_ref),
        ])
    ]
    for load in loads:
        load.start()

    barrier = pltpu.get_barrier_semaphore()
    peers = [{"tp": tp_peer(o, d)} for o, d in others]
    peers += [{"seq": partner, "tp": tp_peer(o, d)} for o, d in everyone]
    peers += [{"seq": before, "tp": tp_peer(o, d)} for o, d in everyone]
    peers += [{"seq": following}, {"seq": plus}, {"seq": minus}]
    peers += [{"seq": z_peer(o)} for o in near]
    for peer in peers:
        pl.semaphore_signal(barrier, inc=1, device_id=peer, device_id_type=pl.DeviceIdType.MESH)

    loads[0].wait()
    loads[1].wait()
    for o in x_order(nx):
        rows = pl.ds(pl.multiple_of(lax.rem(x + o, nx) * 2 * cols, 2 * cols), 2 * cols)
        value = dot(pg_ref[...], up_ref[rows, :], NT)
        if o == 0:
            gm_first[...] = value
        gm_send[o] = value.astype(BF)
    pl.semaphore_wait(barrier, len(peers))
    gm_copies = []
    for k, (o, d) in enumerate(others):
        half = mate_half if d else my_half
        gm_copies.append(send(gm_send.at[o, :, half], gm_recv.at[k], gm_ssem.at[k], gm_rsem.at[k], tp=tp_peer(o, d)))
        gm_copies[-1].start()

    loads[7].wait()
    starts = starts_ref[...].astype(F32)
    slot = lax.broadcasted_iota(jnp.int32, (slots, 1), 0)
    nth = lax.broadcasted_iota(jnp.int32, (slots, pcap), 1)
    lo = jnp.sum(jnp.where(nth == slot, starts, 0.0), axis=1, keepdims=True).astype(jnp.int32)
    lo = jnp.where(slot > pcap, byte_dev, lo)
    after = jnp.where(slot == pcap, 0, slot + 1)
    hi = jnp.sum(jnp.where(nth == after, starts, 0.0), axis=1, keepdims=True).astype(jnp.int32)
    hi = jnp.where((slot > pcap) | (slot == pcap - 1), byte_dev, hi)
    position = lax.broadcasted_iota(jnp.int32, (slots, byte_dev), 1)
    member = (position >= lo) & (position < hi)
    member_bf = jnp.where(member, 1.0, 0.0).astype(BF)
    mt_ref[...] = member_bf.T
    used = (slot < pcap) & (lo < byte_dev)
    owned = jnp.sum(jnp.where(used, 1.0, 0.0), axis=0, keepdims=True).astype(jnp.int32)
    is_prev = slot == pcap
    is_last = slot == owned - 1
    count_own = (hi - lo).astype(F32)

    def exchange(src, dst, ssem, rsem):
        copies = [
            send(src.at[0], dst.at[0], ssem.at[0], rsem.at[0], seq=following),
            send(src.at[1], dst.at[1], ssem.at[1], rsem.at[1], seq=before),
        ]
        for copy in copies:
            copy.start()
        return copies

    loads[2].wait()
    pooled_sum = dot(member_bf, bytes_ref[...])
    for i, mask in enumerate((is_last, is_prev)):
        count_row = jnp.broadcast_to(row_of(mask, count_own), (1, width))
        a_send[i] = rows8(width, row_of(mask, pooled_sum), count_row)
    a_copies = exchange(a_send, a_recv, a_ssem, a_rsem)

    loads[3].wait()
    k_ref[...] = dot(bytes_ref[...], wk_ref[...]).astype(BF)
    loads[4].wait()
    v_ref[...] = dot(bytes_ref[...], wv_ref[...]).astype(BF)

    for copy in gm_copies:
        copy.wait()
    total = gm_first[:, my_half]
    for k in range(len(others)):
        total = total + gm_recv[k].astype(F32)
    mix_own[...] = total.astype(BF)
    shared = pl.ds(pl.multiple_of((rows_dev - window) * (1 - odd), 16), window)
    ag_copies = []
    for k, (o, d) in enumerate(everyone):
        routes = [
            (mix_own.at[shared], pl.ds(rows_dev, window), partner),
            (mix_own.at[pl.ds(rows_dev - 16, 16)], pl.ds(rows_dev + window, 16), following),
        ]
        if (o, d) != (0, 0):
            routes.append((mix_own, pl.ds(0, rows_dev), s))
        for i, (src, rows, seq) in enumerate(routes):
            ag_copies.append(send(
                src, mix_buf.at[rows, mine], ag_ssem.at[i, k], ag_rsem.at[i, k], seq=seq, tp=tp_peer(o, d),
            ))
            ag_copies[-1].start()
    mix_buf[pl.ds(0, rows_dev), mine] = mix_own[...]

    for copy in a_copies:
        copy.wait()
    lane = lax.broadcasted_iota(jnp.int32, (1, cols), 1)
    head0 = lane < HEAD

    def merged(own, received, index):
        width_here = own.shape[1]
        extra = jnp.where(is_prev, received[0, index:index + 1, 0:width_here], 0.0)
        return own + extra + jnp.where(is_last, received[1, index:index + 1, 0:width_here], 0.0)

    pooled_sum = merged(pooled_sum, a_recv, 0)
    counts = jnp.maximum(merged(count_own, a_recv, 1), 1.0)
    pooled_ref[...] = (pooled_sum / counts).astype(BF)
    loads[5].wait()
    queries = dot(pooled_ref[...], wq_ref[...]).astype(BF)

    def heads(value):
        zero = jnp.zeros_like(value)
        return jnp.concatenate([jnp.where(head0, value, zero), jnp.where(head0, zero, value)], axis=0)

    def unheads(value):
        half = value.shape[0] // 2
        return jnp.where(head0, value[:half], value[half:])

    member2 = jnp.concatenate([member, member], axis=0)
    queries2 = heads(queries)
    scores = jnp.where(member2, dot(queries2, k_ref[...], NT) * scale, NEG)
    peak = jnp.max(scores, axis=1, keepdims=True)
    expo = jnp.where(member2, jnp.exp(scores - peak), 0.0)
    expo_bf = expo.astype(BF)
    sums = unheads(jnp.sum(expo, axis=1, keepdims=True))
    peaks = unheads(peak)
    partial_out = unheads(dot(expo_bf, v_ref[...]))
    partial_keys = unheads(dot(expo_bf, k_ref[...]))
    chosen = [
        heads(jnp.broadcast_to(jnp.where(mask, 1.0, 0.0), (slots, cols)).astype(BF)) for mask in (is_last, is_prev)
    ]
    spread = dot(expo_bf, jnp.concatenate(chosen, axis=1), TN)
    values = v_ref[...].astype(F32)
    spread = (spread * jnp.concatenate([values, values], axis=1)).astype(BF)
    products = dot(spread, k_ref[...], TN)
    for i, mask in enumerate((is_last, is_prev)):
        b_send[i, 0:8, :] = rows8(
            cols, row_of(mask, partial_out), row_of(mask, peaks), row_of(mask, sums), row_of(mask, partial_keys),
        )
        b_send[i, 8:8 + HEAD, :] = unheads(products[i * cols:(i + 1) * cols])
    b_copies = exchange(b_send, b_recv, b_ssem, b_rsem)
    bytes_t[...] = bytes_ref[...].T
    pooled_t[...] = pooled_ref[...].T
    for copy in b_copies:
        copy.wait()

    def received(index, empty):
        other = jnp.where(is_last, b_recv[1, index:index + 1, :], empty)
        return jnp.where(is_prev, b_recv[0, index:index + 1, :], other)

    other_peaks = received(1, NEG)
    top = jnp.maximum(peaks, other_peaks)
    keep, add = jnp.exp(peaks - top), jnp.exp(other_peaks - top)
    denom = sums * keep + received(2, 0.0) * add
    denom = jnp.where(denom > 0.0, denom, 1.0)
    attended = ((partial_out * keep + received(0, 0.0) * add) / denom).astype(BF)
    attended2 = heads(attended).astype(F32)
    factor = keep / denom
    factor2 = jnp.concatenate([factor[:, 0:1], factor[:, HEAD:HEAD + 1]], axis=0)
    weights = expo * factor2
    other_factor = add / denom
    base = jnp.where(odd == 0, 0, rows_dev - owned)
    wanted = base + jnp.where(is_prev, -1, slot)
    row = lax.broadcasted_iota(jnp.int32, (slots, rows_dev + window + 16), 1)
    place = jnp.where(row < rows_dev, row, row - odd * (rows_dev + window))
    place = jnp.where(row < rows_dev + window, place, row - (rows_dev + window + 16) - odd * (2 * byte_dev))
    select = jnp.where((place == wanted) & (used | is_prev), 1.0, 0.0).astype(BF)

    def stack(i, value):
        count = width // block
        stack_ref[pl.ds(i * count, count)] = value.astype(BF).reshape(count, block, cols)

    loads[6].wait()
    for copy in ag_copies:
        copy.wait()
    mix_ref[...] = dot(select, mix_buf[...]).astype(BF)
    grad_attended = dot(mix_ref[...], wo_ref[...], NT).astype(BF)
    grad2 = heads(grad_attended)
    delta = jnp.sum(grad2.astype(F32) * attended2, axis=1, keepdims=True)
    grad_scores = (weights * (dot(grad2, v_ref[...], NT) - delta)).astype(BF)
    grad_queries = unheads(dot(grad_scores, k_ref[...]))
    delta = unheads(delta)
    nth = lax.broadcasted_iota(jnp.int32, (HEAD, cols), 0)
    for mask, i in ((is_prev, 0), (is_last, 1)):
        row = row_of(mask, grad_attended.astype(F32))
        column0 = jnp.sum(jnp.where(lane == nth, row, 0.0), axis=1, keepdims=True)
        column1 = jnp.sum(jnp.where(lane == nth + HEAD, row, 0.0), axis=1, keepdims=True)
        whole = jnp.sum(jnp.where(head0, column0, column1) * b_recv[i, 8:8 + HEAD, :], axis=0, keepdims=True)
        whole = whole - row_of(mask, delta) * b_recv[i, 3:4, :]
        grad_queries = grad_queries + jnp.where(mask, row_of(mask, other_factor) * whole, 0.0)
    grad_queries = (grad_queries * scale).astype(BF)
    gk_ref[...] = (dot(grad_scores, queries2, TN) * scale).astype(BF)
    gv_ref[...] = dot(weights.astype(BF), grad2, TN).astype(BF)
    stack(1, dot(bytes_t[...], gk_ref[...]))
    stack(2, dot(bytes_t[...], gv_ref[...]))
    stack(3, dot(mix_ref[...], jnp.where(is_prev, jnp.zeros_like(attended), attended), TN))
    stack(0, dot(pooled_t[...], jnp.where(is_prev, jnp.zeros_like(grad_queries), grad_queries)))

    begins = [sum(len(chunk) for chunk in chunks[:c]) * block for c in range(len(chunks) + 1)]
    opposite, above, below = lax.rem(y + 2, NY), lax.rem(y + 1, NY), lax.rem(y + 3, NY)
    y_copies = {}

    def y_send_to(c, i, src, dst, seq):
        y_copies[c, i] = send(src, dst, y_ssem.at[c, i], y_rsem.at[c, i], seq=seq)
        y_copies[c, i].start()

    def halves(c):
        half = (begins[c + 1] - begins[c]) // 2
        return pl.ds(begins[c], half), pl.ds(begins[c] + half, half)

    def y_first(c):
        for i in range(begins[c] // block, begins[c + 1] // block):
            target = lax.rem(z + order[i] + nz, nz) * NY

            def reorder(q, _, i=i, target=target):
                y_send[q, pl.ds(i * block, block), :] = stack_ref[slots_ref[target + q]]
                return 0

            lax.fori_loop(0, NY, reorder, 0)
        one, two = halves(c)
        y_send_to(c, 0, y_send.at[opposite, one], y_far.at[0, one], plus)
        y_send_to(c, 1, y_send.at[opposite, two], y_far.at[1, two], minus)
        y_send_to(c, 2, y_send.at[above, two], y_dir.at[0, two], plus)
        y_send_to(c, 3, y_send.at[below, one], y_dir.at[1, one], minus)

    def y_second(c):
        one, two = halves(c)
        for i, (rows, q, seq) in enumerate([(one, above, plus), (two, below, minus)]):
            y_copies[c, i].wait_recv()
            value = y_send[q, rows, :].astype(F32) + y_far[i, rows, :].astype(F32)
            y_send[q, rows, :] = value.astype(BF)
            y_send_to(c, 4 + i, y_send.at[q, rows], y_dir.at[i, rows], seq)

    z_copies, far_copies = {}, {}

    def z_rows(o):
        return pl.ds(order.index(o) * block, block)

    def y_sum(c):
        for i in (2, 3, 4, 5):
            y_copies[c, i].wait_recv()
        rows = pl.ds(begins[c], begins[c + 1] - begins[c])
        value = y_send[y, rows, :].astype(F32) + y_dir[0, rows, :].astype(F32) + y_dir[1, rows, :].astype(F32)
        z_send[rows, :] = value.astype(BF)
        for o in chunks[c]:
            if abs(o) > reach:
                i = far.index(o)
                step = o - reach if o > 0 else o + reach
                far_copies[o] = send(
                    z_send.at[z_rows(o)], zf_recv.at[i], zf_ssem.at[i], zf_rsem.at[i], seq=z_peer(step),
                )
                far_copies[o].start()
        for o in sorted((o for o in chunks[c] if 0 < abs(o) <= reach), key=abs):
            if abs(o) == reach:
                value = z_send[z_rows(o), :].astype(F32)
                for i, source in enumerate(far):
                    if (source > 0) == (o > 0):
                        far_copies[source].wait_recv()
                        value = value + zf_recv[i].astype(F32)
                z_send[z_rows(o), :] = value.astype(BF)
            i = near.index(o)
            z_copies[o] = send(z_send.at[z_rows(o)], z_recv.at[i], z_ssem.at[i], z_rsem.at[i], seq=z_peer(o))
            z_copies[o].start()

    p_copies, px_copies = {}, {}

    def p_block(o):
        columns = pl.ds(pl.multiple_of(lax.rem(x + o, nx) * 2 * cols, 2 * cols), 2 * cols)
        value = dot(gk_ref[...], wk_ref[columns, :], NT) + dot(gv_ref[...], wv_ref[columns, :], NT)
        part[o] = (value + dot(mt_ref[...], pb_ref[:, columns])).astype(BF)
        p_copies[o] = send(
            part.at[o, :, mate_half], mate_recv.at[o], p_ssem.at[o], p_rsem.at[o], tp=tp_peer(0, 1),
        )
        p_copies[o].start()

    def p_pair(o):
        p_copies[o].wait_recv()
        return part[o, :, my_half].astype(F32) + mate_recv[o].astype(F32)

    def p_x(o):
        px_send[o - 1] = p_pair(o).astype(BF)
        px_copies[o] = send(
            px_send.at[o - 1], px_recv.at[o - 1], px_ssem.at[o - 1], px_rsem.at[o - 1], tp=tp_peer(o, 0),
        )
        px_copies[o].start()

    loads[8].wait()
    y_first(0)
    y_first(1)
    pb_ref[...] = (dot(grad_queries, wq_ref[...], NT) / counts).astype(BF)
    for step in range(max(nx, len(chunks)) + 1):
        if step < nx:
            p_block(x_order(nx)[step])
        if 0 <= step - 2 < len(chunks):
            y_sum(step - 2)
        if step < len(chunks):
            y_second(step)
        if step + 2 < len(chunks):
            y_first(step + 2)
        if 0 < step < nx:
            p_x(x_order(nx)[step - 1])
    for c in range(max(nx, len(chunks)) - 1, len(chunks)):
        y_sum(c)

    mix_mean = (mix_ref[:, mine].astype(F32) / counts).astype(BF)
    total = p_pair(0) + dot(mt_ref[...], mix_mean)
    for o in px_copies:
        px_copies[o].wait_recv()
        total = total + px_recv[o - 1].astype(F32)
    byte_out[...] = total.astype(BF)

    total = z_send[z_rows(0), :].astype(F32)
    for i, o in enumerate(near):
        z_copies[o].wait_recv()
        total = total + z_recv[i].astype(F32)
    owned_out[...] = total
    for copies in (p_copies, px_copies, y_copies, far_copies, z_copies):
        for copy in copies.values():
            copy.wait_send()


def local(
    byte_states, patch_starts, query_weight, key_weight, value_weight, out_weight, up_weight, patch_grad,
    owner_slots, *, n_seq, ntp,
):
    byte_dev, width = byte_states.shape
    pcap = patch_starts.shape[0]
    rows_dev, features = patch_grad.shape
    cols = query_weight.shape[1]
    slots = up16(pcap + 1)
    window = up16(pcap - rows_dev + 1)
    nz, nx = n_seq // NY, ntp // 2
    order = [o for chunk in z_chunks(nz) for o in chunk]
    near = sum(0 < abs(o) <= nz // 4 for o in order)
    far = nz - 1 - near
    block = 4 * width // n_seq
    vmem = pl.BlockSpec(memory_space=pltpu.VMEM)
    hbm = pl.BlockSpec(memory_space=pltpu.HBM)
    dma = pltpu.SemaphoreType.DMA
    return pl.pallas_call(
        functools.partial(kernel, (n_seq, ntp, pcap, rows_dev, window)),
        out_shape=(
            jax.ShapeDtypeStruct((byte_dev, cols), BF),
            jax.ShapeDtypeStruct((block, cols), F32),
        ),
        in_specs=[hbm] * 9,
        out_specs=(vmem, vmem),
        scratch_shapes=[
            pltpu.VMEM((1, pcap), jnp.int32),
            pltpu.SMEM((n_seq,), jnp.int32),
            pltpu.VMEM((byte_dev, width), BF),
            pltpu.VMEM((width, cols), BF),
            pltpu.VMEM((width, cols), BF),
            pltpu.VMEM((width, cols), BF),
            pltpu.VMEM((cols, width), BF),
            pltpu.VMEM((width, features), BF),
            pltpu.VMEM((rows_dev, features), BF),
            pltpu.VMEM((width, byte_dev), BF),
            pltpu.VMEM((byte_dev, cols), BF),
            pltpu.VMEM((byte_dev, cols), BF),
            pltpu.VMEM((byte_dev, cols), BF),
            pltpu.VMEM((byte_dev, cols), BF),
            pltpu.VMEM((slots, width), BF),
            pltpu.VMEM((width, slots), BF),
            pltpu.VMEM((byte_dev, slots), BF),
            pltpu.VMEM((slots, width), BF),
            pltpu.VMEM((slots, width), BF),
            pltpu.VMEM((n_seq, block, cols), BF),
            pltpu.VMEM((rows_dev, 2 * cols), F32),
            pltpu.VMEM((nx, rows_dev, 2 * cols), BF),
            pltpu.VMEM((ntp - 1, rows_dev, cols), BF),
            pltpu.VMEM((rows_dev, cols), BF),
            pltpu.VMEM((rows_dev + window + 16, width), BF),
            pltpu.VMEM((2, 8, width), F32),
            pltpu.VMEM((2, 8, width), F32),
            pltpu.VMEM((2, 8 + HEAD, cols), F32),
            pltpu.VMEM((2, 8 + HEAD, cols), F32),
            pltpu.VMEM((nx, byte_dev, 2 * cols), BF),
            pltpu.VMEM((nx, byte_dev, cols), BF),
            pltpu.VMEM((nx - 1, byte_dev, cols), BF),
            pltpu.VMEM((nx - 1, byte_dev, cols), BF),
            pltpu.VMEM((NY, nz * block, cols), BF),
            pltpu.VMEM((2, nz * block, cols), BF),
            pltpu.VMEM((2, nz * block, cols), BF),
            pltpu.VMEM((nz * block, cols), BF),
            pltpu.VMEM((far, block, cols), BF),
            pltpu.VMEM((near, block, cols), BF),
            dma((9,)),
            dma((ntp - 1,)), dma((ntp - 1,)),
            dma((3, ntp)), dma((3, ntp)),
            dma((2,)), dma((2,)),
            dma((2,)), dma((2,)),
            dma((nx,)), dma((nx,)),
            dma((nx - 1,)), dma((nx - 1,)),
            dma((4, 6)), dma((4, 6)),
            dma((far,)), dma((far,)),
            dma((near,)), dma((near,)),
        ],
        compiler_params=pltpu.CompilerParams(
            collective_id=0, has_side_effects=True, vmem_limit_bytes=40 * 1024 * 1024
        ),
    )(*[
        pltpu.with_memory_space_constraint(operand, pltpu.HBM)
        for operand in (
            patch_starts.reshape(1, pcap), owner_slots, byte_states, query_weight, key_weight, value_weight,
            out_weight, up_weight, patch_grad,
        )
    ])


def solution(mesh):
    in_specs = (
        P("seq", None),
        P("seq"),
        P(None, "tp"),
        P(None, "tp"),
        P(None, "tp"),
        P("tp", None),
        P(None, "tp"),
        P("seq", "tp"),
        P(),
    )
    out_specs = (P("seq", "tp"), P("seq", "tp"))
    step = functools.partial(local, n_seq=mesh.shape["seq"], ntp=mesh.shape["tp"])
    return jax.shard_map(step, mesh=mesh, in_specs=in_specs, out_specs=out_specs, check_vma=False)
```

```python
import functools

import jax
import jax.numpy as jnp
from jax import lax
from jax.experimental import pallas as pl
from jax.experimental.pallas import tpu as pltpu
from jax.sharding import PartitionSpec as P

HEAD = 64
NY = 4
NEG = -1e30
F32 = jnp.float32
BF = jnp.bfloat16
NT = (((1,), (1,)), ((), ()))
TN = (((0,), (0,)), ((), ()))


def dot(a, b, dims=(((1,), (0,)), ((), ()))):
    return lax.dot_general(a, b, dims, preferred_element_type=F32)


def up16(n):
    return -(-n // 16) * 16


def row_of(mask, value):
    return jnp.sum(jnp.where(mask, value, 0.0), axis=0, keepdims=True)


def rows8(width, *rows):
    index = lax.broadcasted_iota(jnp.int32, (8, width), 0)
    out = jnp.zeros((8, width), F32)
    for i, row in enumerate(rows):
        out = jnp.where(index == i, row, out)
    return out


def z_chunks(nz):
    if nz == 16:
        return [[8, 7, -7], [6, -6, 5, -5], [4, -4, 3, -3], [2, -2, 1, -1, 0]]
    return [[2], [1, -1], [0]]


def x_order(nx):
    return sorted(range(1, nx), key=lambda d: -min(d, nx - d)) + [0]


def kernel(
    sizes,
    starts_hbm, slots_hbm, bytes_hbm, wq_hbm, wk_hbm, wv_hbm, wo_hbm, up_hbm, pg_hbm,
    byte_out, owned_out,
    starts_ref, slots_ref, bytes_ref, wq_ref, wk_ref, wv_ref, wo_ref, up_ref, pg_ref,
    bytes_t, k_ref, v_ref, gk_ref, gv_ref, pooled_ref, pooled_t, mt_ref, mix_ref, pb_ref, stack_ref,
    gm_first, gm_send, gm_recv, mix_own, mix_buf,
    a_send, a_recv, b_send, b_recv,
    part, mate_recv, px_send, px_recv, y_send, y_far, y_dir, z_send, zf_recv, z_recv,
    load_sem, gm_ssem, gm_rsem, ag_ssem, ag_rsem, a_ssem, a_rsem, b_ssem, b_rsem,
    p_ssem, p_rsem, px_ssem, px_rsem, y_ssem, y_rsem, zf_ssem, zf_rsem, z_ssem, z_rsem,
):
    n_seq, ntp, pcap, rows_dev, window = sizes
    nz, nx = n_seq // NY, ntp // 2
    reach = nz // 4
    slots = mt_ref.shape[1]
    byte_dev, width = bytes_ref.shape
    cols = k_ref.shape[1]
    block = owned_out.shape[0]
    scale = HEAD ** -0.5
    s = lax.axis_index("seq")
    t = lax.axis_index("tp")
    y, z = lax.rem(s, NY), s // NY
    x, core = t // 2, lax.rem(t, 2)
    odd = lax.rem(s, 2)
    following, before = lax.rem(s + 1, n_seq), lax.rem(s + n_seq - 1, n_seq)
    partner = s + 1 - 2 * odd
    plus, minus = z * NY + lax.rem(y + 1, NY), z * NY + lax.rem(y + NY - 1, NY)
    chunks = z_chunks(nz)
    order = [o for chunk in chunks for o in chunk]
    near = [o for o in order if 0 < abs(o) <= reach]
    far = [o for o in order if abs(o) > reach]
    mine = pl.ds(pl.multiple_of(t * cols, cols), cols)
    my_half = pl.ds(pl.multiple_of(core * cols, cols), cols)
    mate_half = pl.ds(pl.multiple_of((1 - core) * cols, cols), cols)
    everyone = [(o, d) for o in x_order(nx) for d in (0, 1)]
    others = [pair for pair in everyone if pair != (0, 0)]

    def tp_peer(o, d):
        return 2 * lax.rem(x + o, nx) + lax.rem(core + d, 2)

    def z_peer(o):
        return lax.rem(z + o + nz, nz) * NY + y

    def send(src, dst, ssem, rsem, **where):
        return pltpu.make_async_remote_copy(
            src_ref=src, dst_ref=dst, send_sem=ssem, recv_sem=rsem,
            device_id=where, device_id_type=pl.DeviceIdType.MESH,
        )

    loads = [
        pltpu.make_async_copy(src, dst, load_sem.at[i])
        for i, (src, dst) in enumerate([
            (pg_hbm, pg_ref), (up_hbm, up_ref), (bytes_hbm, bytes_ref), (wk_hbm, wk_ref),
            (wv_hbm, wv_ref), (wq_hbm, wq_ref), (wo_hbm, wo_ref), (starts_hbm, starts_ref), (slots_hbm, slots_ref),
        ])
    ]
    for load in loads:
        load.start()

    barrier = pltpu.get_barrier_semaphore()
    peers = [{"tp": tp_peer(o, d)} for o, d in others]
    peers += [{"seq": partner, "tp": tp_peer(o, d)} for o, d in everyone]
    peers += [{"seq": before, "tp": tp_peer(o, d)} for o, d in everyone]
    peers += [{"seq": following}, {"seq": plus}, {"seq": minus}]
    peers += [{"seq": z_peer(o)} for o in near]
    for peer in peers:
        pl.semaphore_signal(barrier, inc=1, device_id=peer, device_id_type=pl.DeviceIdType.MESH)

    loads[0].wait()
    loads[1].wait()
    for o in x_order(nx):
        rows = pl.ds(pl.multiple_of(lax.rem(x + o, nx) * 2 * cols, 2 * cols), 2 * cols)
        value = dot(pg_ref[...], up_ref[rows, :], NT)
        if o == 0:
            gm_first[...] = value
        gm_send[o] = value.astype(BF)
    pl.semaphore_wait(barrier, len(peers))
    gm_copies = []
    for k, (o, d) in enumerate(others):
        half = mate_half if d else my_half
        gm_copies.append(send(gm_send.at[o, :, half], gm_recv.at[k], gm_ssem.at[k], gm_rsem.at[k], tp=tp_peer(o, d)))
        gm_copies[-1].start()

    loads[7].wait()
    starts = starts_ref[...].astype(F32)
    slot = lax.broadcasted_iota(jnp.int32, (slots, 1), 0)
    nth = lax.broadcasted_iota(jnp.int32, (slots, pcap), 1)
    lo = jnp.sum(jnp.where(nth == slot, starts, 0.0), axis=1, keepdims=True).astype(jnp.int32)
    lo = jnp.where(slot > pcap, byte_dev, lo)
    after = jnp.where(slot == pcap, 0, slot + 1)
    hi = jnp.sum(jnp.where(nth == after, starts, 0.0), axis=1, keepdims=True).astype(jnp.int32)
    hi = jnp.where((slot > pcap) | (slot == pcap - 1), byte_dev, hi)
    position = lax.broadcasted_iota(jnp.int32, (slots, byte_dev), 1)
    member = (position >= lo) & (position < hi)
    member_bf = jnp.where(member, 1.0, 0.0).astype(BF)
    mt_ref[...] = member_bf.T
    used = (slot < pcap) & (lo < byte_dev)
    owned = jnp.sum(jnp.where(used, 1.0, 0.0), axis=0, keepdims=True).astype(jnp.int32)
    is_prev = slot == pcap
    is_last = slot == owned - 1
    count_own = (hi - lo).astype(F32)

    def exchange(src, dst, ssem, rsem):
        copies = [
            send(src.at[0], dst.at[0], ssem.at[0], rsem.at[0], seq=following),
            send(src.at[1], dst.at[1], ssem.at[1], rsem.at[1], seq=before),
        ]
        for copy in copies:
            copy.start()
        return copies

    loads[2].wait()
    pooled_sum = dot(member_bf, bytes_ref[...])
    for i, mask in enumerate((is_last, is_prev)):
        count_row = jnp.broadcast_to(row_of(mask, count_own), (1, width))
        a_send[i] = rows8(width, row_of(mask, pooled_sum), count_row)
    a_copies = exchange(a_send, a_recv, a_ssem, a_rsem)

    loads[3].wait()
    k_ref[...] = dot(bytes_ref[...], wk_ref[...]).astype(BF)
    loads[4].wait()
    v_ref[...] = dot(bytes_ref[...], wv_ref[...]).astype(BF)

    for copy in gm_copies:
        copy.wait()
    total = gm_first[:, my_half]
    for k in range(len(others)):
        total = total + gm_recv[k].astype(F32)
    mix_own[...] = total.astype(BF)
    shared = pl.ds(pl.multiple_of((rows_dev - window) * (1 - odd), 16), window)
    ag_copies = []
    for k, (o, d) in enumerate(everyone):
        routes = [
            (mix_own.at[shared], pl.ds(rows_dev, window), partner),
            (mix_own.at[pl.ds(rows_dev - 16, 16)], pl.ds(rows_dev + window, 16), following),
        ]
        if (o, d) != (0, 0):
            routes.append((mix_own, pl.ds(0, rows_dev), s))
        for i, (src, rows, seq) in enumerate(routes):
            ag_copies.append(send(
                src, mix_buf.at[rows, mine], ag_ssem.at[i, k], ag_rsem.at[i, k], seq=seq, tp=tp_peer(o, d),
            ))
            ag_copies[-1].start()
    mix_buf[pl.ds(0, rows_dev), mine] = mix_own[...]

    for copy in a_copies:
        copy.wait()
    lane = lax.broadcasted_iota(jnp.int32, (1, cols), 1)
    head0 = lane < HEAD

    def merged(own, received, index):
        width_here = own.shape[1]
        extra = jnp.where(is_prev, received[0, index:index + 1, 0:width_here], 0.0)
        return own + extra + jnp.where(is_last, received[1, index:index + 1, 0:width_here], 0.0)

    pooled_sum = merged(pooled_sum, a_recv, 0)
    counts = jnp.maximum(merged(count_own, a_recv, 1), 1.0)
    pooled_ref[...] = (pooled_sum / counts).astype(BF)
    loads[5].wait()
    queries = dot(pooled_ref[...], wq_ref[...]).astype(BF)

    def heads(value):
        zero = jnp.zeros_like(value)
        return jnp.concatenate([jnp.where(head0, value, zero), jnp.where(head0, zero, value)], axis=0)

    def unheads(value):
        half = value.shape[0] // 2
        return jnp.where(head0, value[:half], value[half:])

    member2 = jnp.concatenate([member, member], axis=0)
    queries2 = heads(queries)
    scores = jnp.where(member2, dot(queries2, k_ref[...], NT) * scale, NEG)
    peak = jnp.max(scores, axis=1, keepdims=True)
    expo = jnp.where(member2, jnp.exp(scores - peak), 0.0)
    expo_bf = expo.astype(BF)
    sums = unheads(jnp.sum(expo, axis=1, keepdims=True))
    peaks = unheads(peak)
    partial_out = unheads(dot(expo_bf, v_ref[...]))
    partial_keys = unheads(dot(expo_bf, k_ref[...]))
    chosen = [
        heads(jnp.broadcast_to(jnp.where(mask, 1.0, 0.0), (slots, cols)).astype(BF)) for mask in (is_last, is_prev)
    ]
    spread = dot(expo_bf, jnp.concatenate(chosen, axis=1), TN)
    values = v_ref[...].astype(F32)
    spread = (spread * jnp.concatenate([values, values], axis=1)).astype(BF)
    products = dot(spread, k_ref[...], TN)
    for i, mask in enumerate((is_last, is_prev)):
        b_send[i, 0:8, :] = rows8(
            cols, row_of(mask, partial_out), row_of(mask, peaks), row_of(mask, sums), row_of(mask, partial_keys),
        )
        b_send[i, 8:8 + HEAD, :] = unheads(products[i * cols:(i + 1) * cols])
    b_copies = exchange(b_send, b_recv, b_ssem, b_rsem)
    bytes_t[...] = bytes_ref[...].T
    pooled_t[...] = pooled_ref[...].T
    for copy in b_copies:
        copy.wait()

    def received(index, empty):
        other = jnp.where(is_last, b_recv[1, index:index + 1, :], empty)
        return jnp.where(is_prev, b_recv[0, index:index + 1, :], other)

    other_peaks = received(1, NEG)
    top = jnp.maximum(peaks, other_peaks)
    keep, add = jnp.exp(peaks - top), jnp.exp(other_peaks - top)
    denom = sums * keep + received(2, 0.0) * add
    denom = jnp.where(denom > 0.0, denom, 1.0)
    attended = ((partial_out * keep + received(0, 0.0) * add) / denom).astype(BF)
    attended2 = heads(attended).astype(F32)
    factor = keep / denom
    factor2 = jnp.concatenate([factor[:, 0:1], factor[:, HEAD:HEAD + 1]], axis=0)
    weights = expo * factor2
    other_factor = add / denom
    base = jnp.where(odd == 0, 0, rows_dev - owned)
    wanted = base + jnp.where(is_prev, -1, slot)
    row = lax.broadcasted_iota(jnp.int32, (slots, rows_dev + window + 16), 1)
    place = jnp.where(row < rows_dev, row, row - odd * (rows_dev + window))
    place = jnp.where(row < rows_dev + window, place, row - (rows_dev + window + 16) - odd * (2 * byte_dev))
    select = jnp.where((place == wanted) & (used | is_prev), 1.0, 0.0).astype(BF)

    def stack(i, value):
        count = width // block
        stack_ref[pl.ds(i * count, count)] = value.astype(BF).reshape(count, block, cols)

    loads[6].wait()
    for copy in ag_copies:
        copy.wait()
    mix_ref[...] = dot(select, mix_buf[...]).astype(BF)
    grad_attended = dot(mix_ref[...], wo_ref[...], NT).astype(BF)
    grad2 = heads(grad_attended)
    delta = jnp.sum(grad2.astype(F32) * attended2, axis=1, keepdims=True)
    grad_scores = (weights * (dot(grad2, v_ref[...], NT) - delta)).astype(BF)
    grad_queries = unheads(dot(grad_scores, k_ref[...]))
    delta = unheads(delta)
    nth = lax.broadcasted_iota(jnp.int32, (HEAD, cols), 0)
    for mask, i in ((is_prev, 0), (is_last, 1)):
        row = row_of(mask, grad_attended.astype(F32))
        column0 = jnp.sum(jnp.where(lane == nth, row, 0.0), axis=1, keepdims=True)
        column1 = jnp.sum(jnp.where(lane == nth + HEAD, row, 0.0), axis=1, keepdims=True)
        whole = jnp.sum(jnp.where(head0, column0, column1) * b_recv[i, 8:8 + HEAD, :], axis=0, keepdims=True)
        whole = whole - row_of(mask, delta) * b_recv[i, 3:4, :]
        grad_queries = grad_queries + jnp.where(mask, row_of(mask, other_factor) * whole, 0.0)
    grad_queries = (grad_queries * scale).astype(BF)
    gk_ref[...] = (dot(grad_scores, queries2, TN) * scale).astype(BF)
    gv_ref[...] = dot(weights.astype(BF), grad2, TN).astype(BF)
    stack(1, dot(bytes_t[...], gk_ref[...]))
    stack(2, dot(bytes_t[...], gv_ref[...]))
    stack(3, dot(mix_ref[...], jnp.where(is_prev, jnp.zeros_like(attended), attended), TN))
    stack(0, dot(pooled_t[...], jnp.where(is_prev, jnp.zeros_like(grad_queries), grad_queries)))

    begins = [sum(len(chunk) for chunk in chunks[:c]) * block for c in range(len(chunks) + 1)]
    opposite, above, below = lax.rem(y + 2, NY), lax.rem(y + 1, NY), lax.rem(y + 3, NY)
    y_copies = {}

    def y_send_to(c, i, src, dst, seq):
        y_copies[c, i] = send(src, dst, y_ssem.at[c, i], y_rsem.at[c, i], seq=seq)
        y_copies[c, i].start()

    def halves(c):
        half = (begins[c + 1] - begins[c]) // 2
        return pl.ds(begins[c], half), pl.ds(begins[c] + half, half)

    def y_first(c):
        for i in range(begins[c] // block, begins[c + 1] // block):
            target = lax.rem(z + order[i] + nz, nz) * NY

            def reorder(q, _, i=i, target=target):
                y_send[q, pl.ds(i * block, block), :] = stack_ref[slots_ref[target + q]]
                return 0

            lax.fori_loop(0, NY, reorder, 0)
        one, two = halves(c)
        y_send_to(c, 0, y_send.at[opposite, one], y_far.at[0, one], plus)
        y_send_to(c, 1, y_send.at[opposite, two], y_far.at[1, two], minus)
        y_send_to(c, 2, y_send.at[above, two], y_dir.at[0, two], plus)
        y_send_to(c, 3, y_send.at[below, one], y_dir.at[1, one], minus)

    def y_second(c):
        one, two = halves(c)
        for i, (rows, q, seq) in enumerate([(one, above, plus), (two, below, minus)]):
            y_copies[c, i].wait_recv()
            value = y_send[q, rows, :].astype(F32) + y_far[i, rows, :].astype(F32)
            y_send[q, rows, :] = value.astype(BF)
            y_send_to(c, 4 + i, y_send.at[q, rows], y_dir.at[i, rows], seq)

    z_copies, far_copies = {}, {}

    def z_rows(o):
        return pl.ds(order.index(o) * block, block)

    def y_sum(c):
        for i in (2, 3, 4, 5):
            y_copies[c, i].wait_recv()
        rows = pl.ds(begins[c], begins[c + 1] - begins[c])
        value = y_send[y, rows, :].astype(F32) + y_dir[0, rows, :].astype(F32) + y_dir[1, rows, :].astype(F32)
        z_send[rows, :] = value.astype(BF)
        for o in chunks[c]:
            if abs(o) > reach:
                i = far.index(o)
                step = o - reach if o > 0 else o + reach
                far_copies[o] = send(
                    z_send.at[z_rows(o)], zf_recv.at[i], zf_ssem.at[i], zf_rsem.at[i], seq=z_peer(step),
                )
                far_copies[o].start()
        for o in sorted((o for o in chunks[c] if 0 < abs(o) <= reach), key=abs):
            if abs(o) == reach:
                value = z_send[z_rows(o), :].astype(F32)
                for i, source in enumerate(far):
                    if (source > 0) == (o > 0):
                        far_copies[source].wait_recv()
                        value = value + zf_recv[i].astype(F32)
                z_send[z_rows(o), :] = value.astype(BF)
            i = near.index(o)
            z_copies[o] = send(z_send.at[z_rows(o)], z_recv.at[i], z_ssem.at[i], z_rsem.at[i], seq=z_peer(o))
            z_copies[o].start()

    p_copies, px_copies = {}, {}

    def p_block(o):
        columns = pl.ds(pl.multiple_of(lax.rem(x + o, nx) * 2 * cols, 2 * cols), 2 * cols)
        value = dot(gk_ref[...], wk_ref[columns, :], NT) + dot(gv_ref[...], wv_ref[columns, :], NT)
        part[o] = (value + dot(mt_ref[...], pb_ref[:, columns])).astype(BF)
        p_copies[o] = send(
            part.at[o, :, mate_half], mate_recv.at[o], p_ssem.at[o], p_rsem.at[o], tp=tp_peer(0, 1),
        )
        p_copies[o].start()

    def p_pair(o):
        p_copies[o].wait_recv()
        return part[o, :, my_half].astype(F32) + mate_recv[o].astype(F32)

    def p_x(o):
        px_send[o - 1] = p_pair(o).astype(BF)
        px_copies[o] = send(
            px_send.at[o - 1], px_recv.at[o - 1], px_ssem.at[o - 1], px_rsem.at[o - 1], tp=tp_peer(o, 0),
        )
        px_copies[o].start()

    loads[8].wait()
    y_first(0)
    y_first(1)
    y_first(2)
    pb_ref[...] = (dot(grad_queries, wq_ref[...], NT) / counts).astype(BF)
    y_second(0)
    p_block(2)
    y_second(1)
    y_first(3)
    p_block(1)
    y_sum(0)
    y_second(2)
    p_x(2)
    p_block(3)
    y_sum(1)
    y_second(3)
    p_x(1)
    p_block(0)
    p_x(3)
    y_sum(2)
    y_sum(3)

    mix_mean = (mix_ref[:, mine].astype(F32) / counts).astype(BF)
    total = p_pair(0) + dot(mt_ref[...], mix_mean)
    for o in px_copies:
        px_copies[o].wait_recv()
        total = total + px_recv[o - 1].astype(F32)
    byte_out[...] = total.astype(BF)

    total = z_send[z_rows(0), :].astype(F32)
    for i, o in enumerate(near):
        z_copies[o].wait_recv()
        total = total + z_recv[i].astype(F32)
    owned_out[...] = total
    for copies in (p_copies, px_copies, y_copies, far_copies, z_copies):
        for copy in copies.values():
            copy.wait_send()


def local(
    byte_states, patch_starts, query_weight, key_weight, value_weight, out_weight, up_weight, patch_grad,
    owner_slots, *, n_seq, ntp,
):
    byte_dev, width = byte_states.shape
    pcap = patch_starts.shape[0]
    rows_dev, features = patch_grad.shape
    cols = query_weight.shape[1]
    slots = up16(pcap + 1)
    window = up16(pcap - rows_dev + 1)
    nz, nx = n_seq // NY, ntp // 2
    order = [o for chunk in z_chunks(nz) for o in chunk]
    near = sum(0 < abs(o) <= nz // 4 for o in order)
    far = nz - 1 - near
    block = 4 * width // n_seq
    vmem = pl.BlockSpec(memory_space=pltpu.VMEM)
    hbm = pl.BlockSpec(memory_space=pltpu.HBM)
    dma = pltpu.SemaphoreType.DMA
    return pl.pallas_call(
        functools.partial(kernel, (n_seq, ntp, pcap, rows_dev, window)),
        out_shape=(
            jax.ShapeDtypeStruct((byte_dev, cols), BF),
            jax.ShapeDtypeStruct((block, cols), F32),
        ),
        in_specs=[hbm] * 9,
        out_specs=(vmem, vmem),
        scratch_shapes=[
            pltpu.VMEM((1, pcap), jnp.int32),
            pltpu.SMEM((n_seq,), jnp.int32),
            pltpu.VMEM((byte_dev, width), BF),
            pltpu.VMEM((width, cols), BF),
            pltpu.VMEM((width, cols), BF),
            pltpu.VMEM((width, cols), BF),
            pltpu.VMEM((cols, width), BF),
            pltpu.VMEM((width, features), BF),
            pltpu.VMEM((rows_dev, features), BF),
            pltpu.VMEM((width, byte_dev), BF),
            pltpu.VMEM((byte_dev, cols), BF),
            pltpu.VMEM((byte_dev, cols), BF),
            pltpu.VMEM((byte_dev, cols), BF),
            pltpu.VMEM((byte_dev, cols), BF),
            pltpu.VMEM((slots, width), BF),
            pltpu.VMEM((width, slots), BF),
            pltpu.VMEM((byte_dev, slots), BF),
            pltpu.VMEM((slots, width), BF),
            pltpu.VMEM((slots, width), BF),
            pltpu.VMEM((n_seq, block, cols), BF),
            pltpu.VMEM((rows_dev, 2 * cols), F32),
            pltpu.VMEM((nx, rows_dev, 2 * cols), BF),
            pltpu.VMEM((ntp - 1, rows_dev, cols), BF),
            pltpu.VMEM((rows_dev, cols), BF),
            pltpu.VMEM((rows_dev + window + 16, width), BF),
            pltpu.VMEM((2, 8, width), F32),
            pltpu.VMEM((2, 8, width), F32),
            pltpu.VMEM((2, 8 + HEAD, cols), F32),
            pltpu.VMEM((2, 8 + HEAD, cols), F32),
            pltpu.VMEM((nx, byte_dev, 2 * cols), BF),
            pltpu.VMEM((nx, byte_dev, cols), BF),
            pltpu.VMEM((nx - 1, byte_dev, cols), BF),
            pltpu.VMEM((nx - 1, byte_dev, cols), BF),
            pltpu.VMEM((NY, nz * block, cols), BF),
            pltpu.VMEM((2, nz * block, cols), BF),
            pltpu.VMEM((2, nz * block, cols), BF),
            pltpu.VMEM((nz * block, cols), BF),
            pltpu.VMEM((far, block, cols), BF),
            pltpu.VMEM((near, block, cols), BF),
            dma((9,)),
            dma((ntp - 1,)), dma((ntp - 1,)),
            dma((3, ntp)), dma((3, ntp)),
            dma((2,)), dma((2,)),
            dma((2,)), dma((2,)),
            dma((nx,)), dma((nx,)),
            dma((nx - 1,)), dma((nx - 1,)),
            dma((4, 6)), dma((4, 6)),
            dma((far,)), dma((far,)),
            dma((near,)), dma((near,)),
        ],
        compiler_params=pltpu.CompilerParams(
            collective_id=0, has_side_effects=True, vmem_limit_bytes=40 * 1024 * 1024
        ),
    )(*[
        pltpu.with_memory_space_constraint(operand, pltpu.HBM)
        for operand in (
            patch_starts.reshape(1, pcap), owner_slots, byte_states, query_weight, key_weight, value_weight,
            out_weight, up_weight, patch_grad,
        )
    ])


def solution(mesh):
    in_specs = (
        P("seq", None),
        P("seq"),
        P(None, "tp"),
        P(None, "tp"),
        P(None, "tp"),
        P("tp", None),
        P(None, "tp"),
        P("seq", "tp"),
        P(),
    )
    out_specs = (P("seq", "tp"), P("seq", "tp"))
    step = functools.partial(local, n_seq=mesh.shape["seq"], ntp=mesh.shape["tp"])
    return jax.shard_map(step, mesh=mesh, in_specs=in_specs, out_specs=out_specs, check_vma=False)
```

```python
import functools

import jax
import jax.numpy as jnp
from jax import lax
from jax.experimental import pallas as pl
from jax.experimental.pallas import tpu as pltpu
from jax.sharding import PartitionSpec as P

HEAD = 64
NY = 4
NEG = -1e30
F32 = jnp.float32
BF = jnp.bfloat16
NT = (((1,), (1,)), ((), ()))
TN = (((0,), (0,)), ((), ()))


def dot(a, b, dims=(((1,), (0,)), ((), ()))):
    return lax.dot_general(a, b, dims, preferred_element_type=F32)


def up16(n):
    return -(-n // 16) * 16


def row_of(mask, value):
    return jnp.sum(jnp.where(mask, value, 0.0), axis=0, keepdims=True)


def rows8(width, *rows):
    index = lax.broadcasted_iota(jnp.int32, (8, width), 0)
    out = jnp.zeros((8, width), F32)
    for i, row in enumerate(rows):
        out = jnp.where(index == i, row, out)
    return out


def z_chunks(nz):
    if nz == 16:
        return [[8, 7, -7], [6, -6, 5, -5], [4, -4, 3, -3], [2, -2, 1, -1, 0]]
    return [[2], [1, -1], [0]]


def x_order(nx):
    return sorted(range(1, nx), key=lambda d: -min(d, nx - d)) + [0]


def kernel(
    sizes,
    starts_hbm, slots_hbm, bytes_hbm, wq_hbm, wk_hbm, wv_hbm, wo_hbm, up_hbm, pg_hbm,
    byte_out, owned_out,
    starts_ref, slots_ref, bytes_ref, wq_ref, wk_ref, wv_ref, wo_ref, up_ref, pg_ref,
    bytes_t, k_ref, v_ref, gk_ref, gv_ref, pooled_ref, pooled_t, mt_ref, mix_ref, pb_ref, stack_ref,
    gm_first, gm_send, gm_recv, mix_own, mix_buf,
    a_send, a_recv, b_send, b_recv,
    part, mate_recv, px_send, px_recv, y_send, y_far, y_dir, z_send, zf_recv, z_recv,
    load_sem, gm_ssem, gm_rsem, ag_ssem, ag_rsem, a_ssem, a_rsem, b_ssem, b_rsem,
    p_ssem, p_rsem, px_ssem, px_rsem, y_ssem, y_rsem, zf_ssem, zf_rsem, z_ssem, z_rsem,
):
    n_seq, ntp, pcap, rows_dev, window = sizes
    nz, nx = n_seq // NY, ntp // 2
    reach = nz // 4
    slots = mt_ref.shape[1]
    byte_dev, width = bytes_ref.shape
    cols = k_ref.shape[1]
    block = owned_out.shape[0]
    scale = HEAD ** -0.5
    s = lax.axis_index("seq")
    t = lax.axis_index("tp")
    y, z = lax.rem(s, NY), s // NY
    x, core = t // 2, lax.rem(t, 2)
    odd = lax.rem(s, 2)
    following, before = lax.rem(s + 1, n_seq), lax.rem(s + n_seq - 1, n_seq)
    partner = s + 1 - 2 * odd
    plus, minus = z * NY + lax.rem(y + 1, NY), z * NY + lax.rem(y + NY - 1, NY)
    chunks = z_chunks(nz)
    order = [o for chunk in chunks for o in chunk]
    near = [o for o in order if 0 < abs(o) <= reach]
    far = [o for o in order if abs(o) > reach]
    mine = pl.ds(pl.multiple_of(t * cols, cols), cols)
    my_half = pl.ds(pl.multiple_of(core * cols, cols), cols)
    mate_half = pl.ds(pl.multiple_of((1 - core) * cols, cols), cols)
    everyone = [(o, d) for o in x_order(nx) for d in (0, 1)]
    others = [pair for pair in everyone if pair != (0, 0)]

    def tp_peer(o, d):
        return 2 * lax.rem(x + o, nx) + lax.rem(core + d, 2)

    def z_peer(o):
        return lax.rem(z + o + nz, nz) * NY + y

    def send(src, dst, ssem, rsem, **where):
        return pltpu.make_async_remote_copy(
            src_ref=src, dst_ref=dst, send_sem=ssem, recv_sem=rsem,
            device_id=where, device_id_type=pl.DeviceIdType.MESH,
        )

    loads = [
        pltpu.make_async_copy(src, dst, load_sem.at[i])
        for i, (src, dst) in enumerate([
            (pg_hbm, pg_ref), (up_hbm, up_ref), (bytes_hbm, bytes_ref), (wk_hbm, wk_ref),
            (wv_hbm, wv_ref), (wq_hbm, wq_ref), (wo_hbm, wo_ref), (starts_hbm, starts_ref), (slots_hbm, slots_ref),
        ])
    ]
    barrier = pltpu.get_barrier_semaphore()
    peers = [{"tp": tp_peer(o, d)} for o, d in others]
    peers += [{"seq": partner, "tp": tp_peer(o, d)} for o, d in everyone]
    peers += [{"seq": before, "tp": tp_peer(o, d)} for o, d in everyone]
    peers += [{"seq": following}, {"seq": plus}, {"seq": minus}]
    peers += [{"seq": z_peer(o)} for o in near]
    for peer in reversed(peers):
        pl.semaphore_signal(barrier, inc=1, device_id=peer, device_id_type=pl.DeviceIdType.MESH)

    for load in loads:
        load.start()

    loads[0].wait()
    loads[1].wait()
    for o in x_order(nx):
        rows = pl.ds(pl.multiple_of(lax.rem(x + o, nx) * 2 * cols, 2 * cols), 2 * cols)
        value = dot(pg_ref[...], up_ref[rows, :], NT)
        if o == 0:
            gm_first[...] = value
        gm_send[o] = value.astype(BF)
    pl.semaphore_wait(barrier, len(peers))
    gm_copies = []
    for k, (o, d) in enumerate(others):
        half = mate_half if d else my_half
        gm_copies.append(send(gm_send.at[o, :, half], gm_recv.at[k], gm_ssem.at[k], gm_rsem.at[k], tp=tp_peer(o, d)))
        gm_copies[-1].start()

    loads[7].wait()
    starts = starts_ref[...].astype(F32)
    slot = lax.broadcasted_iota(jnp.int32, (slots, 1), 0)
    nth = lax.broadcasted_iota(jnp.int32, (slots, pcap), 1)
    lo = jnp.sum(jnp.where(nth == slot, starts, 0.0), axis=1, keepdims=True).astype(jnp.int32)
    lo = jnp.where(slot > pcap, byte_dev, lo)
    after = jnp.where(slot == pcap, 0, slot + 1)
    hi = jnp.sum(jnp.where(nth == after, starts, 0.0), axis=1, keepdims=True).astype(jnp.int32)
    hi = jnp.where((slot > pcap) | (slot == pcap - 1), byte_dev, hi)
    position = lax.broadcasted_iota(jnp.int32, (slots, byte_dev), 1)
    member = (position >= lo) & (position < hi)
    member_bf = jnp.where(member, 1.0, 0.0).astype(BF)
    mt_ref[...] = member_bf.T
    used = (slot < pcap) & (lo < byte_dev)
    owned = jnp.sum(jnp.where(used, 1.0, 0.0), axis=0, keepdims=True).astype(jnp.int32)
    is_prev = slot == pcap
    is_last = slot == owned - 1
    count_own = (hi - lo).astype(F32)

    def exchange(src, dst, ssem, rsem):
        copies = [
            send(src.at[0], dst.at[0], ssem.at[0], rsem.at[0], seq=following),
            send(src.at[1], dst.at[1], ssem.at[1], rsem.at[1], seq=before),
        ]
        for copy in copies:
            copy.start()
        return copies

    loads[2].wait()
    pooled_sum = dot(member_bf, bytes_ref[...])
    for i, mask in enumerate((is_last, is_prev)):
        count_row = jnp.broadcast_to(row_of(mask, count_own), (1, width))
        a_send[i] = rows8(width, row_of(mask, pooled_sum), count_row)
    a_copies = exchange(a_send, a_recv, a_ssem, a_rsem)

    loads[3].wait()
    k_ref[...] = dot(bytes_ref[...], wk_ref[...]).astype(BF)
    loads[4].wait()
    v_ref[...] = dot(bytes_ref[...], wv_ref[...]).astype(BF)

    for copy in gm_copies:
        copy.wait()
    total = gm_first[:, my_half]
    for k in range(len(others)):
        total = total + gm_recv[k].astype(F32)
    mix_own[...] = total.astype(BF)
    shared = pl.ds(pl.multiple_of((rows_dev - window) * (1 - odd), 16), window)
    ag_copies = []
    for k, (o, d) in enumerate(everyone):
        routes = [
            (mix_own.at[shared], pl.ds(rows_dev, window), partner),
            (mix_own.at[pl.ds(rows_dev - 16, 16)], pl.ds(rows_dev + window, 16), following),
        ]
        if (o, d) != (0, 0):
            routes.append((mix_own, pl.ds(0, rows_dev), s))
        for i, (src, rows, seq) in enumerate(routes):
            ag_copies.append(send(
                src, mix_buf.at[rows, mine], ag_ssem.at[i, k], ag_rsem.at[i, k], seq=seq, tp=tp_peer(o, d),
            ))
            ag_copies[-1].start()
    mix_buf[pl.ds(0, rows_dev), mine] = mix_own[...]

    for copy in a_copies:
        copy.wait()
    lane = lax.broadcasted_iota(jnp.int32, (1, cols), 1)
    head0 = lane < HEAD

    def merged(own, received, index):
        width_here = own.shape[1]
        extra = jnp.where(is_prev, received[0, index:index + 1, 0:width_here], 0.0)
        return own + extra + jnp.where(is_last, received[1, index:index + 1, 0:width_here], 0.0)

    pooled_sum = merged(pooled_sum, a_recv, 0)
    counts = jnp.maximum(merged(count_own, a_recv, 1), 1.0)
    pooled_ref[...] = (pooled_sum / counts).astype(BF)
    loads[5].wait()
    queries = dot(pooled_ref[...], wq_ref[...]).astype(BF)

    def heads(value):
        zero = jnp.zeros_like(value)
        return jnp.concatenate([jnp.where(head0, value, zero), jnp.where(head0, zero, value)], axis=0)

    def unheads(value):
        half = value.shape[0] // 2
        return jnp.where(head0, value[:half], value[half:])

    member2 = jnp.concatenate([member, member], axis=0)
    queries2 = heads(queries)
    scores = jnp.where(member2, dot(queries2, k_ref[...], NT) * scale, NEG)
    peak = jnp.max(scores, axis=1, keepdims=True)
    expo = jnp.where(member2, jnp.exp(scores - peak), 0.0)
    expo_bf = expo.astype(BF)
    sums = unheads(jnp.sum(expo, axis=1, keepdims=True))
    peaks = unheads(peak)
    partial_out = unheads(dot(expo_bf, v_ref[...]))
    partial_keys = unheads(dot(expo_bf, k_ref[...]))
    chosen = [
        heads(jnp.broadcast_to(jnp.where(mask, 1.0, 0.0), (slots, cols)).astype(BF)) for mask in (is_last, is_prev)
    ]
    spread = dot(expo_bf, jnp.concatenate(chosen, axis=1), TN)
    values = v_ref[...].astype(F32)
    spread = (spread * jnp.concatenate([values, values], axis=1)).astype(BF)
    products = dot(spread, k_ref[...], TN)
    for i, mask in enumerate((is_last, is_prev)):
        b_send[i, 0:8, :] = rows8(
            cols, row_of(mask, partial_out), row_of(mask, peaks), row_of(mask, sums), row_of(mask, partial_keys),
        )
        b_send[i, 8:8 + HEAD, :] = unheads(products[i * cols:(i + 1) * cols])
    b_copies = exchange(b_send, b_recv, b_ssem, b_rsem)
    bytes_t[...] = bytes_ref[...].T
    pooled_t[...] = pooled_ref[...].T
    for copy in b_copies:
        copy.wait()

    def received(index, empty):
        other = jnp.where(is_last, b_recv[1, index:index + 1, :], empty)
        return jnp.where(is_prev, b_recv[0, index:index + 1, :], other)

    other_peaks = received(1, NEG)
    top = jnp.maximum(peaks, other_peaks)
    keep, add = jnp.exp(peaks - top), jnp.exp(other_peaks - top)
    denom = sums * keep + received(2, 0.0) * add
    denom = jnp.where(denom > 0.0, denom, 1.0)
    attended = ((partial_out * keep + received(0, 0.0) * add) / denom).astype(BF)
    attended2 = heads(attended).astype(F32)
    factor = keep / denom
    factor2 = jnp.concatenate([factor[:, 0:1], factor[:, HEAD:HEAD + 1]], axis=0)
    weights = expo * factor2
    other_factor = add / denom
    base = jnp.where(odd == 0, 0, rows_dev - owned)
    wanted = base + jnp.where(is_prev, -1, slot)
    row = lax.broadcasted_iota(jnp.int32, (slots, rows_dev + window + 16), 1)
    place = jnp.where(row < rows_dev, row, row - odd * (rows_dev + window))
    place = jnp.where(row < rows_dev + window, place, row - (rows_dev + window + 16) - odd * (2 * byte_dev))
    select = jnp.where((place == wanted) & (used | is_prev), 1.0, 0.0).astype(BF)

    def stack(i, value):
        count = width // block
        stack_ref[pl.ds(i * count, count)] = value.astype(BF).reshape(count, block, cols)

    loads[6].wait()
    for copy in ag_copies:
        copy.wait()
    mix_ref[...] = dot(select, mix_buf[...]).astype(BF)
    grad_attended = dot(mix_ref[...], wo_ref[...], NT).astype(BF)
    grad2 = heads(grad_attended)
    delta = jnp.sum(grad2.astype(F32) * attended2, axis=1, keepdims=True)
    grad_scores = (weights * (dot(grad2, v_ref[...], NT) - delta)).astype(BF)
    grad_queries = unheads(dot(grad_scores, k_ref[...]))
    delta = unheads(delta)
    nth = lax.broadcasted_iota(jnp.int32, (HEAD, cols), 0)
    for mask, i in ((is_prev, 0), (is_last, 1)):
        row = row_of(mask, grad_attended.astype(F32))
        column0 = jnp.sum(jnp.where(lane == nth, row, 0.0), axis=1, keepdims=True)
        column1 = jnp.sum(jnp.where(lane == nth + HEAD, row, 0.0), axis=1, keepdims=True)
        whole = jnp.sum(jnp.where(head0, column0, column1) * b_recv[i, 8:8 + HEAD, :], axis=0, keepdims=True)
        whole = whole - row_of(mask, delta) * b_recv[i, 3:4, :]
        grad_queries = grad_queries + jnp.where(mask, row_of(mask, other_factor) * whole, 0.0)
    grad_queries = (grad_queries * scale).astype(BF)
    gk_ref[...] = (dot(grad_scores, queries2, TN) * scale).astype(BF)
    gv_ref[...] = dot(weights.astype(BF), grad2, TN).astype(BF)
    stack(1, dot(bytes_t[...], gk_ref[...]))
    stack(2, dot(bytes_t[...], gv_ref[...]))
    stack(3, dot(mix_ref[...], jnp.where(is_prev, jnp.zeros_like(attended), attended), TN))
    stack(0, dot(pooled_t[...], jnp.where(is_prev, jnp.zeros_like(grad_queries), grad_queries)))

    begins = [sum(len(chunk) for chunk in chunks[:c]) * block for c in range(len(chunks) + 1)]
    opposite, above, below = lax.rem(y + 2, NY), lax.rem(y + 1, NY), lax.rem(y + 3, NY)
    y_copies = {}

    def y_send_to(c, i, src, dst, seq):
        y_copies[c, i] = send(src, dst, y_ssem.at[c, i], y_rsem.at[c, i], seq=seq)
        y_copies[c, i].start()

    def halves(c):
        half = (begins[c + 1] - begins[c]) // 2
        return pl.ds(begins[c], half), pl.ds(begins[c] + half, half)

    def y_first(c):
        for i in range(begins[c] // block, begins[c + 1] // block):
            target = lax.rem(z + order[i] + nz, nz) * NY

            def reorder(q, _, i=i, target=target):
                y_send[q, pl.ds(i * block, block), :] = stack_ref[slots_ref[target + q]]
                return 0

            lax.fori_loop(0, NY, reorder, 0)
        one, two = halves(c)
        y_send_to(c, 0, y_send.at[opposite, one], y_far.at[0, one], plus)
        y_send_to(c, 1, y_send.at[opposite, two], y_far.at[1, two], minus)
        y_send_to(c, 2, y_send.at[above, two], y_dir.at[0, two], plus)
        y_send_to(c, 3, y_send.at[below, one], y_dir.at[1, one], minus)

    def y_second(c):
        one, two = halves(c)
        for i, (rows, q, seq) in enumerate([(one, above, plus), (two, below, minus)]):
            y_copies[c, i].wait_recv()
            value = y_send[q, rows, :].astype(F32) + y_far[i, rows, :].astype(F32)
            y_send[q, rows, :] = value.astype(BF)
            y_send_to(c, 4 + i, y_send.at[q, rows], y_dir.at[i, rows], seq)

    z_copies, far_copies = {}, {}

    def z_rows(o):
        return pl.ds(order.index(o) * block, block)

    def y_sum(c):
        for i in (2, 3, 4, 5):
            y_copies[c, i].wait_recv()
        rows = pl.ds(begins[c], begins[c + 1] - begins[c])
        value = y_send[y, rows, :].astype(F32) + y_dir[0, rows, :].astype(F32) + y_dir[1, rows, :].astype(F32)
        z_send[rows, :] = value.astype(BF)
        for o in chunks[c]:
            if abs(o) > reach:
                i = far.index(o)
                step = o - reach if o > 0 else o + reach
                far_copies[o] = send(
                    z_send.at[z_rows(o)], zf_recv.at[i], zf_ssem.at[i], zf_rsem.at[i], seq=z_peer(step),
                )
                far_copies[o].start()
        for o in sorted((o for o in chunks[c] if 0 < abs(o) <= reach), key=abs):
            if abs(o) == reach:
                value = z_send[z_rows(o), :].astype(F32)
                for i, source in enumerate(far):
                    if (source > 0) == (o > 0):
                        far_copies[source].wait_recv()
                        value = value + zf_recv[i].astype(F32)
                z_send[z_rows(o), :] = value.astype(BF)
            i = near.index(o)
            z_copies[o] = send(z_send.at[z_rows(o)], z_recv.at[i], z_ssem.at[i], z_rsem.at[i], seq=z_peer(o))
            z_copies[o].start()

    p_copies, px_copies = {}, {}

    def p_block(o):
        columns = pl.ds(pl.multiple_of(lax.rem(x + o, nx) * 2 * cols, 2 * cols), 2 * cols)
        value = dot(gk_ref[...], wk_ref[columns, :], NT) + dot(gv_ref[...], wv_ref[columns, :], NT)
        part[o] = (value + dot(mt_ref[...], pb_ref[:, columns])).astype(BF)
        p_copies[o] = send(
            part.at[o, :, mate_half], mate_recv.at[o], p_ssem.at[o], p_rsem.at[o], tp=tp_peer(0, 1),
        )
        p_copies[o].start()

    def p_pair(o):
        p_copies[o].wait_recv()
        return part[o, :, my_half].astype(F32) + mate_recv[o].astype(F32)

    def p_x(o):
        px_send[o - 1] = p_pair(o).astype(BF)
        px_copies[o] = send(
            px_send.at[o - 1], px_recv.at[o - 1], px_ssem.at[o - 1], px_rsem.at[o - 1], tp=tp_peer(o, 0),
        )
        px_copies[o].start()

    loads[8].wait()
    y_first(0)
    y_first(1)
    y_first(2)
    pb_ref[...] = (dot(grad_queries, wq_ref[...], NT) / counts).astype(BF)
    y_second(0)
    p_block(2)
    y_second(1)
    y_first(3)
    p_block(1)
    y_sum(0)
    y_second(2)
    p_x(2)
    p_block(3)
    y_sum(1)
    y_second(3)
    p_x(1)
    p_block(0)
    p_x(3)
    y_sum(2)
    y_sum(3)

    mix_mean = (mix_ref[:, mine].astype(F32) / counts).astype(BF)
    total = p_pair(0) + dot(mt_ref[...], mix_mean)
    for o in px_copies:
        px_copies[o].wait_recv()
        total = total + px_recv[o - 1].astype(F32)
    byte_out[...] = total.astype(BF)

    total = z_send[z_rows(0), :].astype(F32)
    for i, o in enumerate(near):
        z_copies[o].wait_recv()
        total = total + z_recv[i].astype(F32)
    owned_out[...] = total
    for copies in (p_copies, px_copies, y_copies, far_copies, z_copies):
        for copy in copies.values():
            copy.wait_send()


def local(
    byte_states, patch_starts, query_weight, key_weight, value_weight, out_weight, up_weight, patch_grad,
    owner_slots, *, n_seq, ntp,
):
    byte_dev, width = byte_states.shape
    pcap = patch_starts.shape[0]
    rows_dev, features = patch_grad.shape
    cols = query_weight.shape[1]
    slots = up16(pcap + 1)
    window = up16(pcap - rows_dev + 1)
    nz, nx = n_seq // NY, ntp // 2
    order = [o for chunk in z_chunks(nz) for o in chunk]
    near = sum(0 < abs(o) <= nz // 4 for o in order)
    far = nz - 1 - near
    block = 4 * width // n_seq
    vmem = pl.BlockSpec(memory_space=pltpu.VMEM)
    hbm = pl.BlockSpec(memory_space=pltpu.HBM)
    dma = pltpu.SemaphoreType.DMA
    return pl.pallas_call(
        functools.partial(kernel, (n_seq, ntp, pcap, rows_dev, window)),
        out_shape=(
            jax.ShapeDtypeStruct((byte_dev, cols), BF),
            jax.ShapeDtypeStruct((block, cols), F32),
        ),
        in_specs=[hbm] * 9,
        out_specs=(vmem, vmem),
        scratch_shapes=[
            pltpu.VMEM((1, pcap), jnp.int32),
            pltpu.SMEM((n_seq,), jnp.int32),
            pltpu.VMEM((byte_dev, width), BF),
            pltpu.VMEM((width, cols), BF),
            pltpu.VMEM((width, cols), BF),
            pltpu.VMEM((width, cols), BF),
            pltpu.VMEM((cols, width), BF),
            pltpu.VMEM((width, features), BF),
            pltpu.VMEM((rows_dev, features), BF),
            pltpu.VMEM((width, byte_dev), BF),
            pltpu.VMEM((byte_dev, cols), BF),
            pltpu.VMEM((byte_dev, cols), BF),
            pltpu.VMEM((byte_dev, cols), BF),
            pltpu.VMEM((byte_dev, cols), BF),
            pltpu.VMEM((slots, width), BF),
            pltpu.VMEM((width, slots), BF),
            pltpu.VMEM((byte_dev, slots), BF),
            pltpu.VMEM((slots, width), BF),
            pltpu.VMEM((slots, width), BF),
            pltpu.VMEM((n_seq, block, cols), BF),
            pltpu.VMEM((rows_dev, 2 * cols), F32),
            pltpu.VMEM((nx, rows_dev, 2 * cols), BF),
            pltpu.VMEM((ntp - 1, rows_dev, cols), BF),
            pltpu.VMEM((rows_dev, cols), BF),
            pltpu.VMEM((rows_dev + window + 16, width), BF),
            pltpu.VMEM((2, 8, width), F32),
            pltpu.VMEM((2, 8, width), F32),
            pltpu.VMEM((2, 8 + HEAD, cols), F32),
            pltpu.VMEM((2, 8 + HEAD, cols), F32),
            pltpu.VMEM((nx, byte_dev, 2 * cols), BF),
            pltpu.VMEM((nx, byte_dev, cols), BF),
            pltpu.VMEM((nx - 1, byte_dev, cols), BF),
            pltpu.VMEM((nx - 1, byte_dev, cols), BF),
            pltpu.VMEM((NY, nz * block, cols), BF),
            pltpu.VMEM((2, nz * block, cols), BF),
            pltpu.VMEM((2, nz * block, cols), BF),
            pltpu.VMEM((nz * block, cols), BF),
            pltpu.VMEM((far, block, cols), BF),
            pltpu.VMEM((near, block, cols), BF),
            dma((9,)),
            dma((ntp - 1,)), dma((ntp - 1,)),
            dma((3, ntp)), dma((3, ntp)),
            dma((2,)), dma((2,)),
            dma((2,)), dma((2,)),
            dma((nx,)), dma((nx,)),
            dma((nx - 1,)), dma((nx - 1,)),
            dma((4, 6)), dma((4, 6)),
            dma((far,)), dma((far,)),
            dma((near,)), dma((near,)),
        ],
        compiler_params=pltpu.CompilerParams(
            collective_id=0, has_side_effects=True, vmem_limit_bytes=40 * 1024 * 1024
        ),
    )(*[
        pltpu.with_memory_space_constraint(operand, pltpu.HBM)
        for operand in (
            patch_starts.reshape(1, pcap), owner_slots, byte_states, query_weight, key_weight, value_weight,
            out_weight, up_weight, patch_grad,
        )
    ])


def solution(mesh):
    in_specs = (
        P("seq", None),
        P("seq"),
        P(None, "tp"),
        P(None, "tp"),
        P(None, "tp"),
        P("tp", None),
        P(None, "tp"),
        P("seq", "tp"),
        P(),
    )
    out_specs = (P("seq", "tp"), P("seq", "tp"))
    step = functools.partial(local, n_seq=mesh.shape["seq"], ntp=mesh.shape["tp"])
    return jax.shard_map(step, mesh=mesh, in_specs=in_specs, out_specs=out_specs, check_vma=False)
```
